256 devices in a mesh: row: 8 (over z), col: 16 (over x, y), rep: 2 (over core).
Axes of the slice: x: 4, y: 4, z: 8, core: 2. Of those that a mesh axis runs over, the one named last changes fastest.
Arguments:
- gradients: float32 [2, 8192, 8192], P('rep', ('row', 'col')), may hold values from -6 to 6
- momentum: float32 [8192, 8192], P(('row', 'rep'), 'col'), may hold values from -6 to 6
- right_basis: float32 [8192, 1024], P('col'), may hold values from -0.0625 to 0.0625
Outputs:
- new_momentum: float32 [8192, 8192], P(('row', 'rep'), 'col')
- new_basis: float32 [8192, 1024], P('col')
- update: float32 [8192, 8192], P(('row', 'rep'), 'col')
The draws below stay inside these ranges and needn't reach their ends.
All inputs are finite; a program needn't handle non-finite values.
Results may differ from the reference program's by a relative error of at most 0.00014.
Values sent between devices are 32-bit elements; how exact they have to be, the bound alone decides.
A program may use at most 128 MiB of HBM per device.

```python
import math
import jax
import jax.numpy as jnp
from jax import lax

D = 8192
RANK = 1024
REPLICAS = 2


def level_of(own_key, extent, shards, least, top_value):
    def one(position, parts):
        draws = jax.random.uniform(jax.random.fold_in(jax.random.fold_in(own_key, 6), position), (parts,), jnp.float32, least / len(shards), top_value / len(shards))
        return jnp.repeat(jnp.exp(draws), extent[position] // parts).reshape((-1,) + (1,) * (len(extent) - position - 1))

    factor_of = one(*shards[0])
    for cut in shards[1:]:
        factor_of = factor_of * one(*cut)
    return factor_of


def bell_draw(stream_key, extent, deviation, most, pieces=(), kind=jnp.bfloat16):
    array = deviation * jax.random.normal(stream_key, extent, jnp.float32)
    if pieces:
        array = array * level_of(stream_key, extent, pieces, -0.22, 0.18)
    return jnp.clip(array, -most, most).astype(kind)


def setup_inputs(seed: int = 0) -> dict:
    seeds = jax.random.split(jax.random.key(seed), 4)
    gradients = bell_draw(seeds[0], (REPLICAS, D, D), 1.0, 6.0, ((0, 2), (1, 128)), jnp.float32)
    momentum = bell_draw(seeds[1], (D, D), 1.0, 6.0, ((0, 16), (1, 16)), jnp.float32)
    right_basis = bell_draw(seeds[2], (D, RANK), D ** -0.5, 0.0625, ((0, 16),), jnp.float32)
    return dict(gradients=gradients, momentum=momentum, right_basis=right_basis)


EPSILON = 1e-06
RIDGE = 0.001
DECAY = 0.95

def reference(gradients, momentum, right_basis):
    high = lax.Precision.HIGHEST
    summed = lax.optimization_barrier(jnp.sum(gradients, axis=0))
    buffer = momentum + summed
    left_panel = jnp.dot(buffer.astype(jnp.float32), right_basis.astype(jnp.float32), precision=high, preferred_element_type=jnp.float32)
    gram = jnp.dot(left_panel.T.astype(jnp.float32), left_panel.astype(jnp.float32), precision=high, preferred_element_type=jnp.float32)
    gram = gram + RIDGE * jnp.eye(gram.shape[0], dtype=gram.dtype)
    factor = jnp.linalg.cholesky(gram)
    left_unit = lax.linalg.triangular_solve(factor, left_panel, left_side=False, lower=True, transpose_a=True)
    right_panel = jnp.dot(buffer.T.astype(jnp.float32), left_unit.astype(jnp.float32), precision=high, preferred_element_type=jnp.float32)
    right_norm = jnp.sqrt(lax.optimization_barrier(jnp.sum(right_panel * right_panel, axis=0, keepdims=True)) + EPSILON)
    new_basis = right_panel / right_norm
    new_momentum = buffer - (1.0 - DECAY) * jnp.dot(left_unit.astype(jnp.float32), right_panel.T.astype(jnp.float32), precision=high, preferred_element_type=jnp.float32)
    scale = D / math.sqrt(RANK)
    update = scale * jnp.dot(left_unit.astype(jnp.float32), new_basis.T.astype(jnp.float32), precision=high, preferred_element_type=jnp.float32)
    return (new_momentum, new_basis, update)
```

```python
import functools
import math

import jax, jax.numpy as jnp
from jax import lax
from jax.experimental import pallas as pl
from jax.experimental.pallas import tpu as pltpu
from jax.sharding import PartitionSpec as P

N = 1024
NB = 128
HI = lax.Precision.HIGHEST


def factor_block(rows):
    nr = len(rows)
    rows = list(rows)
    lane = lax.broadcasted_iota(jnp.int32, (8, NB), 1)
    sub = lax.broadcasted_iota(jnp.int32, (8, NB), 0)

    def lanes(v, j):
        return jnp.broadcast_to(v[:, j : j + 1], (8, NB))

    def subs(v, k):
        return jnp.broadcast_to(v[k : k + 1, :], (8, NB))

    for J in range(nr):
        blk = (lane >= 8 * J) & (lane < 8 * J + 8)
        V = rows[J]
        C = [lanes(V, 8 * J + k) for k in range(8)]
        D = {i: [lanes(rows[i], 8 * J + k) for k in range(8)] for i in range(J + 1, nr)}
        V = jnp.where(blk, jnp.where(lane - 8 * J == sub, 1.0, 0.0), V)
        for i in range(J + 1, nr):
            rows[i] = jnp.where(blk, 0.0, rows[i])
        for k in range(8):
            s = lax.rsqrt(subs(C[k], k))
            vk = subs(V, k) * s
            f = jnp.where(sub > k, C[k] * s, 0.0)
            V = jnp.where(sub == k, vk, V - f * vk)
            ck = {}
            for q in range(k + 1, 8):
                ck[q] = subs(C[q], k) * s
                C[q] = C[q] - f * ck[q]
            for i in range(J + 1, nr):
                fi = D[i][k] * s
                rows[i] = rows[i] - fi * vk
                for q in range(k + 1, 8):
                    D[i][q] = D[i][q] - fi * ck[q]
        rows[J] = V
    return rows


def chol_kernel(g_ref, x_ref, ridge, prec=HI):
    nb = N // NB
    r = lax.broadcasted_iota(jnp.int32, (NB, NB), 0)
    c = lax.broadcasted_iota(jnp.int32, (NB, NB), 1)
    x_ref[...] = g_ref[...]

    def step(k, _):
        kr = pl.ds(pl.multiple_of(k * NB, NB), NB)
        rows = [x_ref[pl.ds(pl.multiple_of(k * NB + 8 * i, 8), 8), kr] for i in range(NB // 8)]
        eye8 = [jnp.where(lax.broadcasted_iota(jnp.int32, (8, NB), 0) + 8 * i == lax.broadcasted_iota(jnp.int32, (8, NB), 1), ridge, 0.0) for i in range(NB // 8)]
        rows = [a + b for a, b in zip(rows, eye8)]
        rows = factor_block(rows)
        res = jnp.concatenate(rows, axis=0)
        dinv = jnp.where(r >= c, res, 0.0)
        x_ref[kr, kr] = jnp.where(r == c, 1.0, 0.0)
        rs = lax.dot_general(dinv, x_ref[kr, :], (((1,), (0,)), ((), ())), precision=prec, preferred_element_type=jnp.float32)
        x_ref[kr, :] = rs

        def trail(i, _):
            ir = pl.ds(pl.multiple_of(i * NB, NB), NB)
            f = x_ref[kr, ir]
            x_ref[ir, kr] = jnp.zeros((NB, NB), jnp.float32)
            x_ref[ir, :] = x_ref[ir, :] - lax.dot_general(f, x_ref[kr, :], (((0,), (0,)), ((), ())), precision=prec, preferred_element_type=jnp.float32)
            return 0

        lax.fori_loop(k + 1, nb, trail, 0)
        return 0

    lax.fori_loop(0, nb, step, 0)


def chol_inv(g, ridge):
    return pl.pallas_call(
        functools.partial(chol_kernel, ridge=ridge),
        out_shape=jax.ShapeDtypeStruct((N, N), jnp.float32),
        in_specs=[pl.BlockSpec(memory_space=pltpu.VMEM)],
        out_specs=pl.BlockSpec(memory_space=pltpu.VMEM),
        cost_estimate=pl.CostEstimate(flops=100_000_000_000, bytes_accessed=8 << 20, transcendentals=0),
        compiler_params=pltpu.CompilerParams(vmem_limit_bytes=40 << 20),
    )(g)


EPSILON = 1e-06
RIDGE = 0.001
DECAY = 0.95
D = 8192


def dot(left, right, dims, precision=HI):
    return lax.dot_general(left, right, (dims, ((), ())), precision=precision, preferred_element_type=jnp.float32)


def shards(gradients, momentum, right_basis):
    slab = gradients[0]
    regrid = lax.all_to_all(slab, "col", split_axis=1, concat_axis=0, tiled=True)
    summed = lax.psum_scatter(regrid, "rep", scatter_dimension=0, tiled=True)
    buffer = momentum + summed
    left_panel = lax.psum(dot(buffer, right_basis, ((1,), (0,))), "col")
    share = N // lax.axis_size("col")
    mine = lax.dynamic_slice_in_dim(left_panel, lax.axis_index("col") * share, share, 1)
    gram_share = lax.psum(dot(mine, left_panel, ((0,), (0,))), ("row", "rep"))
    gram = lax.all_gather(gram_share, "col", axis=0, tiled=True)
    partial_cross, gram = lax.optimization_barrier((dot(buffer, left_panel, ((0,), (0,))), gram))
    cross_panel = lax.psum(partial_cross, ("row", "rep"))
    low = jnp.tril(chol_inv(gram, RIDGE))
    left_unit = dot(left_panel, low, ((1,), (1,)))
    right_panel = dot(cross_panel, low, ((1,), (1,)))
    squares = lax.psum(jnp.sum(right_panel * right_panel, axis=0, keepdims=True), "col")
    new_basis = right_panel / jnp.sqrt(squares + EPSILON)
    new_momentum = buffer - (1.0 - DECAY) * dot(left_unit, right_panel, ((1,), (1,)))
    update = (D / math.sqrt(N)) * dot(left_unit, new_basis, ((1,), (1,)))
    return (new_momentum, new_basis, update)


def solution(mesh):
    return jax.shard_map(
        shards,
        mesh=mesh,
        in_specs=(P("rep", ("row", "col"), None), P(("row", "rep"), "col"), P("col", None)),
        out_specs=(P(("row", "rep"), "col"), P("col", None), P(("row", "rep"), "col")),
        check_vma=False,
    )
```

```python
import functools
import math

import jax, jax.numpy as jnp
from jax import lax
from jax.experimental import pallas as pl
from jax.experimental.pallas import tpu as pltpu
from jax.sharding import PartitionSpec as P

N = 1024
NB = 128
HI = lax.Precision.HIGHEST


def factor_block(rows):
    nr = len(rows)
    rows = list(rows)
    lane = lax.broadcasted_iota(jnp.int32, (8, NB), 1)
    sub = lax.broadcasted_iota(jnp.int32, (8, NB), 0)

    def lanes(v, j):
        return jnp.broadcast_to(v[:, j : j + 1], (8, NB))

    def subs(v, k):
        return jnp.broadcast_to(v[k : k + 1, :], (8, NB))

    for J in range(nr):
        blk = (lane >= 8 * J) & (lane < 8 * J + 8)
        V = rows[J]
        C = [lanes(V, 8 * J + k) for k in range(8)]
        D = {i: [lanes(rows[i], 8 * J + k) for k in range(8)] for i in range(J + 1, nr)}
        V = jnp.where(blk, jnp.where(lane - 8 * J == sub, 1.0, 0.0), V)
        for i in range(J + 1, nr):
            rows[i] = jnp.where(blk, 0.0, rows[i])
        for k in range(8):
            s = lax.rsqrt(subs(C[k], k))
            vk = subs(V, k) * s
            f = jnp.where(sub > k, C[k] * s, 0.0)
            V = jnp.where(sub == k, vk, V - f * vk)
            ck = {}
            for q in range(k + 1, 8):
                ck[q] = subs(C[q], k) * s
                C[q] = C[q] - f * ck[q]
            for i in range(J + 1, nr):
                fi = D[i][k] * s
                rows[i] = rows[i] - fi * vk
                for q in range(k + 1, 8):
                    D[i][q] = D[i][q] - fi * ck[q]
        rows[J] = V
    return rows


def chol_kernel(g_ref, x_ref, ridge, prec=HI):
    nb = N // NB
    r = lax.broadcasted_iota(jnp.int32, (NB, NB), 0)
    c = lax.broadcasted_iota(jnp.int32, (NB, NB), 1)
    x_ref[...] = g_ref[...]

    def step(k, _):
        kr = pl.ds(pl.multiple_of(k * NB, NB), NB)
        rows = [x_ref[pl.ds(pl.multiple_of(k * NB + 8 * i, 8), 8), kr] for i in range(NB // 8)]
        eye8 = [jnp.where(lax.broadcasted_iota(jnp.int32, (8, NB), 0) + 8 * i == lax.broadcasted_iota(jnp.int32, (8, NB), 1), ridge, 0.0) for i in range(NB // 8)]
        rows = [a + b for a, b in zip(rows, eye8)]
        rows = factor_block(rows)
        res = jnp.concatenate(rows, axis=0)
        dinv = jnp.where(r >= c, res, 0.0)
        x_ref[kr, kr] = jnp.where(r == c, 1.0, 0.0)
        rs = lax.dot_general(dinv, x_ref[kr, :], (((1,), (0,)), ((), ())), precision=prec, preferred_element_type=jnp.float32)
        x_ref[kr, :] = rs

        def trail(i, _):
            ir = pl.ds(pl.multiple_of(i * NB, NB), NB)
            f = x_ref[kr, ir]
            x_ref[ir, kr] = jnp.zeros((NB, NB), jnp.float32)
            x_ref[ir, :] = x_ref[ir, :] - lax.dot_general(f, x_ref[kr, :], (((0,), (0,)), ((), ())), precision=prec, preferred_element_type=jnp.float32)
            return 0

        lax.fori_loop(k + 1, nb, trail, 0)
        return 0

    lax.fori_loop(0, nb, step, 0)


def chol_inv(g, ridge):
    return pl.pallas_call(
        functools.partial(chol_kernel, ridge=ridge),
        out_shape=jax.ShapeDtypeStruct((N, N), jnp.float32),
        in_specs=[pl.BlockSpec(memory_space=pltpu.VMEM)],
        out_specs=pl.BlockSpec(memory_space=pltpu.VMEM),
        cost_estimate=pl.CostEstimate(flops=100_000_000_000, bytes_accessed=8 << 20, transcendentals=0),
        compiler_params=pltpu.CompilerParams(vmem_limit_bytes=40 << 20),
    )(g)


MESH = pl.DeviceIdType.MESH


def dot(left, right, dims, precision=HI):
    return lax.dot_general(left, right, (dims, ((), ())), precision=precision, preferred_element_type=jnp.float32)


def remote(src, dst, send, recv, device):
    return pltpu.make_async_remote_copy(
        src_ref=src, dst_ref=dst, send_sem=send, recv_sem=recv, device_id=device, device_id_type=MESH
    )


def ring_scatter(piece, half, from_a, from_b, from_left, from_right, pos, left, right, send, recv, started):
    before, after, across = (pos + 3) % 4, (pos + 1) % 4, (pos + 2) % 4
    a = remote(half(across, 0), from_a, send.at[0], recv.at[0], left)
    b = remote(half(across, 1), from_b, send.at[1], recv.at[1], right)
    a.start()
    b.start()
    yield
    a.wait_recv()
    half(before, 0)[...] = half(before, 0)[...] + from_a[...]
    c = remote(piece(before), from_right, send.at[2], recv.at[2], left)
    c.start()
    b.wait_recv()
    half(after, 1)[...] = half(after, 1)[...] + from_b[...]
    d = remote(piece(after), from_left, send.at[3], recv.at[3], right)
    d.start()
    yield
    c.wait_recv()
    d.wait_recv()
    piece(pos)[...] = piece(pos)[...] + (from_left[...] + from_right[...])
    started += [a, b, c, d]


def ring_gather(piece, half, pos, left, right, send, recv, started, done=None):
    before, after, across = (pos + 3) % 4, (pos + 1) % 4, (pos + 2) % 4
    a = remote(piece(pos), piece(pos), send.at[0], recv.at[0], left)
    b = remote(piece(pos), piece(pos), send.at[1], recv.at[1], right)
    a.start()
    b.start()
    if done:
        done(0, pos)
    yield
    a.wait_recv()
    c = remote(half(after, 0), half(after, 0), send.at[2], recv.at[2], left)
    c.start()
    b.wait_recv()
    d = remote(half(before, 1), half(before, 1), send.at[3], recv.at[3], right)
    d.start()
    if done:
        done(1, after)
        done(2, before)
    yield
    c.wait_recv()
    d.wait_recv()
    if done:
        done(3, across)
    started += [a, b, c, d]


def lockstep(*stages):
    stages = list(stages)
    while stages:
        for stage in list(stages):
            try:
                next(stage)
            except StopIteration:
                stages.remove(stage)


def front_kernel(
    slab, momentum, basis,
    gram, buffer, left_panel, cross_half,
    part, total, landed, panel, from_a, from_b, from_left, from_right, from_a2, from_b2, from_left2, from_right2, full,
    gram_part, gram_in, gram_slots, gram_sum, gram_all, cross_part, cross_in,
    part_send, part_recv, land_send, land_recv, ring_send, ring_recv, z_send, z_recv, pair_send, pair_recv,
):
    r, c, p = lax.axis_index("row"), lax.axis_index("col"), lax.axis_index("rep")
    x, y = c // 4, c % 4
    mate = (r, c, 1 - p)
    sides = {
        "x": ((r, ((x + 3) % 4) * 4 + y, p), (r, ((x + 1) % 4) * 4 + y, p)),
        "y": ((r, x * 4 + (y + 3) % 4, p), (r, x * 4 + (y + 1) % 4, p)),
    }
    alone = (c // 8 == p) & (c % 2 == p)

    barrier = pltpu.get_barrier_semaphore()
    pl.semaphore_signal(barrier, inc=1, device_id=mate, device_id_type=MESH)
    for axis in ("x", "y"):
        for side in sides[axis]:
            pl.semaphore_signal(barrier, inc=1, device_id=side, device_id_type=MESH)
    for step in range(1, 8):
        pl.semaphore_signal(barrier, inc=1, device_id=((r + step) % 8, c, p), device_id_type=MESH)
    for slot in range(8):
        @pl.when(jnp.logical_not(alone & (8 * p + slot == c)))
        def _():
            pl.semaphore_signal(barrier, inc=1, device_id=(r, 8 * p + slot, c % 2), device_id_type=MESH)
    pl.semaphore_wait(barrier, jnp.where(alone, 19, 20))

    started = []

    first = c // 2
    copies = []
    for step in range(8):
        b = (first + step) % 8
        cols = pl.ds(pl.multiple_of(512 * (2 * b + 1 - p), 512), 512)
        copy = remote(slab.at[0, :, cols], part.at[step], part_send.at[step], part_recv.at[step], mate)
        copy.start()
        copies.append(copy)
    started += copies
    for step in range(8):
        b = (first + step) % 8
        d = 2 * b + p
        copies[step].wait_recv()
        cols = pl.ds(pl.multiple_of(512 * d, 512), 512)
        total[step] = part[step] + slab[0, :, cols]
        own = (d == c) & (c // 8 == p)

        @pl.when(own)
        def _():
            landed[c % 8] = total[step]

        @pl.when(jnp.logical_not(own))
        def _():
            remote(total.at[step], landed.at[c % 8], land_send.at[step], land_recv.at[c % 8], (r, d, c // 8)).start()

    for slot in range(8):
        @pl.when(jnp.logical_not(alone & (8 * p + slot == c)))
        def _():
            remote(total.at[0], landed.at[slot], land_send.at[0], land_recv.at[slot], (r, 8 * p + slot, c % 2)).wait_recv()
        buffer[64 * slot : 64 * slot + 64, :] = momentum[64 * slot : 64 * slot + 64, :] + landed[slot]

    across = {"x": (x + 2) % 4, "y": (y + 2) % 4}
    where = {"x": x, "y": y}

    def product(h):
        axis = "xy"[h]
        for t in range(4):
            if h == 0:
                rows = buffer[128 * t : 128 * t + 128, :]
            else:
                rows = jnp.concatenate([buffer[32 * (4 * u + t) : 32 * (4 * u + t) + 32, :] for u in range(4)], axis=0)
            got = dot(rows, basis[:, 512 * h : 512 * h + 512], ((1,), (0,)))
            for u in range(4):
                panel[h, t, u] = got[32 * u : 32 * u + 32]

    def scatter(h):
        axis, other = ("x", "y") if h == 0 else ("y", "x")
        product(h)
        yield from ring_scatter(
            lambda i: panel.at[h, i],
            lambda i, k: panel.at[h, i, pl.ds(2 * k, 2)],
            from_a.at[h], from_b.at[h], from_left.at[h], from_right.at[h],
            where[axis], *sides[axis], ring_send.at[h, 0], ring_recv.at[h, 0], started,
        )
        yield
        yield from ring_scatter(
            lambda i: panel.at[h, where[axis], i],
            lambda i, k: panel.at[h, where[axis], i, pl.ds(16 * k, 16)],
            from_a2.at[h], from_b2.at[h], from_left2.at[h], from_right2.at[h],
            where[other], *sides[other], ring_send.at[h, 1], ring_recv.at[h, 1], started,
        )
        full[h, where[axis], where[other]] = panel[h, where[axis], where[other]]
        yield
        yield from ring_gather(
            lambda i: full.at[h, where[axis], i],
            lambda i, k: full.at[h, where[axis], i, pl.ds(16 * k, 16)],
            where[other], *sides[other], ring_send.at[h, 2], ring_recv.at[h, 2], started,
        )
        yield
        yield from ring_gather(
            lambda i: full.at[h, i],
            lambda i, k: full.at[h, i, pl.ds(2 * k, 2)],
            where[axis], *sides[axis], ring_send.at[h, 3], ring_recv.at[h, 3], started,
        )

    lockstep(scatter(0), scatter(1))
    for u in range(4):
        for v in range(4):
            rows = slice(32 * (4 * u + v), 32 * (4 * u + v) + 32)
            left_panel[rows, 0:512] = full[0, u, v]
            left_panel[rows, 512:1024] = full[1, v, u]

    rows = pl.ds(pl.multiple_of(128 * (c // 2), 128), 128)
    mine = left_panel[:, rows]
    for q in range(2):
        cols = pl.ds(pl.multiple_of(512 * (c % 2) + 256 * q, 256), 256)
        gram_part[q] = dot(mine, left_panel[:, cols], ((0,), (0,)))
    swap = remote(gram_part.at[1 - p], gram_in, pair_send.at[8], pair_recv.at[8], mate)
    swap.start()
    started.append(swap)

    for q in range(2):
        cross_part[q] = dot(buffer[:, 256 * q : 256 * q + 256], left_panel[...], ((0,), (0,)))
    cross_swap = remote(cross_part.at[1 - p], cross_in, pair_send.at[9], pair_recv.at[9], mate)
    cross_swap.start()
    started.append(cross_swap)

    swap.wait_recv()
    gram_part[p] = gram_part[p] + gram_in[...]
    moves = []
    for step in range(1, 8):
        z = (r + step) % 8
        piece = gram_part.at[p, pl.ds(pl.multiple_of(16 * z, 16), 16)]
        move = remote(piece, gram_slots.at[r], z_send.at[0, step], z_recv.at[0, step], (z, c, p))
        move.start()
        moves.append(move)
    gram_slots[r] = gram_part[p, pl.ds(pl.multiple_of(16 * r, 16), 16)]
    started += moves
    for move in moves:
        move.wait_recv()
    acc = gram_slots[0]
    for z in range(1, 8):
        acc = acc + gram_slots[z]
    h = r // 4
    f, s = jnp.where(h == 0, x, y), jnp.where(h == 0, y, x)
    place = gram_all.at[p, h, f, s, pl.ds(pl.multiple_of(16 * (r % 4), 16), 16)]
    gram_sum[...] = acc
    place[...] = acc
    moves = []
    for step in range(1, 8):
        move = remote(gram_sum, place, z_send.at[1, step], z_recv.at[1, step], ((r + step) % 8, c, p))
        move.start()
        moves.append(move)
    started += moves
    for move in moves:
        move.wait_recv()

    pairs = []

    def gather(h):
        axis, other = ("x", "y") if h == 0 else ("y", "x")
        yield from ring_gather(
            lambda i: gram_all.at[p, h, where[axis], i],
            lambda i, k: gram_all.at[p, h, where[axis], i, pl.ds(32 * k, 32)],
            where[other], *sides[other], ring_send.at[h, 4], ring_recv.at[h, 4], started,
        )
        yield

        def forward(k, i):
            view = gram_all.at[p, h, i]
            copy = remote(view, view, pair_send.at[4 * h + k], pair_recv.at[4 * h + k], mate)
            copy.start()
            pairs.append(copy)

        yield from ring_gather(
            lambda i: gram_all.at[p, h, i],
            lambda i, k: gram_all.at[p, h, i, pl.ds(2 * k, 2)],
            where[axis], *sides[axis], ring_send.at[h, 5], ring_recv.at[h, 5], started, forward,
        )

    lockstep(gather(0), gather(1))
    for copy in pairs:
        copy.wait_recv()
    started += pairs
    for q in range(2):
        for u in range(4):
            for v in range(4):
                n = 4 * u + v
                cols = slice(512 * (n % 2) + 256 * q, 512 * (n % 2) + 256 * q + 256)
                top = 128 * (n // 2)
                gram[top : top + 64, cols] = gram_all[q, 0, u, v]
                gram[top + 64 : top + 128, cols] = gram_all[q, 1, v, u]

    cross_swap.wait_recv()
    cross_half[...] = cross_part[p] + cross_in[...]
    for copy in started:
        copy.wait_send()
    for step in range(8):
        b = (first + step) % 8
        d = 2 * b + p

        @pl.when(jnp.logical_not((d == c) & (c // 8 == p)))
        def _():
            remote(total.at[step], landed.at[c % 8], land_send.at[step], land_recv.at[c % 8], (r, d, c // 8)).wait_send()


def front(gradients, momentum, right_basis):
    f32 = jnp.float32
    vmem = pl.BlockSpec(memory_space=pltpu.VMEM)
    dma = pltpu.SemaphoreType.DMA
    return pl.pallas_call(
        front_kernel,
        out_shape=[
            jax.ShapeDtypeStruct((N, N), f32),
            jax.ShapeDtypeStruct((512, 512), f32),
            jax.ShapeDtypeStruct((512, N), f32),
            jax.ShapeDtypeStruct((256, N), f32),
        ],
        in_specs=[vmem] * 3,
        out_specs=[vmem] * 4,
        scratch_shapes=[
            pltpu.VMEM((8, 64, 512), f32),
            pltpu.VMEM((8, 64, 512), f32),
            pltpu.VMEM((8, 64, 512), f32),
            pltpu.VMEM((2, 4, 4, 32, 512), f32),
            pltpu.VMEM((2, 2, 32, 512), f32),
            pltpu.VMEM((2, 2, 32, 512), f32),
            pltpu.VMEM((2, 4, 32, 512), f32),
            pltpu.VMEM((2, 4, 32, 512), f32),
            pltpu.VMEM((2, 16, 512), f32),
            pltpu.VMEM((2, 16, 512), f32),
            pltpu.VMEM((2, 32, 512), f32),
            pltpu.VMEM((2, 32, 512), f32),
            pltpu.VMEM((2, 4, 4, 32, 512), f32),
            pltpu.VMEM((2, 128, 256), f32),
            pltpu.VMEM((128, 256), f32),
            pltpu.VMEM((8, 16, 256), f32),
            pltpu.VMEM((16, 256), f32),
            pltpu.VMEM((2, 2, 4, 4, 64, 256), f32),
            pltpu.VMEM((2, 256, N), f32),
            pltpu.VMEM((256, N), f32),
            dma((8,)), dma((8,)), dma((8,)), dma((8,)),
            dma((2, 6, 4)), dma((2, 6, 4)),
            dma((2, 8)), dma((2, 8)),
            dma((10,)), dma((10,)),
        ],
        compiler_params=pltpu.CompilerParams(
            collective_id=0, has_side_effects=True, vmem_limit_bytes=50 << 20
        ),
    )(gradients, momentum, right_basis)


EPSILON = 1e-06
RIDGE = 0.001
DECAY = 0.95
D = 8192


def shards(gradients, momentum, right_basis):
    gram, buffer, left_panel, cross_half = front(gradients, momentum, right_basis)
    cross_rows = lax.psum(cross_half, "row")
    cross_panel = lax.all_gather(cross_rows, "rep", axis=0, tiled=True)
    low = jnp.tril(chol_inv(gram, RIDGE))
    left_unit = dot(left_panel, low, ((1,), (1,)))
    right_panel = dot(cross_panel, low, ((1,), (1,)))
    squares = lax.psum(jnp.sum(right_panel * right_panel, axis=0, keepdims=True), "col")
    new_basis = right_panel / jnp.sqrt(squares + EPSILON)
    new_momentum = buffer - (1.0 - DECAY) * dot(left_unit, right_panel, ((1,), (1,)))
    update = (D / math.sqrt(N)) * dot(left_unit, new_basis, ((1,), (1,)))
    return (new_momentum, new_basis, update)


def solution(mesh):
    return jax.shard_map(
        shards,
        mesh=mesh,
        in_specs=(P("rep", ("row", "col"), None), P(("row", "rep"), "col"), P("col", None)),
        out_specs=(P(("row", "rep"), "col"), P("col", None), P(("row", "rep"), "col")),
        check_vma=False,
    )
```

```python
import functools
import math

import jax
import jax.numpy as jnp
from jax import lax
from jax.experimental import pallas as pl
from jax.experimental.pallas import tpu as pltpu
from jax.sharding import PartitionSpec as P

N = 1024
NB = 128
HI = lax.Precision.HIGHEST
EPSILON = 1e-06
RIDGE = 0.001
DECAY = 0.95
D = 8192
MESH = pl.DeviceIdType.MESH


def dot(left, right, dims, precision=HI):
    return lax.dot_general(left, right, (dims, ((), ())), precision=precision, preferred_element_type=jnp.float32)


def split(a):
    high = a.astype(jnp.bfloat16)
    return high, (a - high.astype(jnp.float32)).astype(jnp.bfloat16)


def dot3(left, right, dims):
    def one(a, b):
        return lax.dot_general(a, b, (dims, ((), ())), preferred_element_type=jnp.float32)

    return one(left[0], right[0]) + (one(left[0], right[1]) + one(left[1], right[0]))


def remote(src, dst, send, recv, device):
    return pltpu.make_async_remote_copy(
        src_ref=src, dst_ref=dst, send_sem=send, recv_sem=recv, device_id=device, device_id_type=MESH
    )


def factor_block(rest):
    lane = lax.broadcasted_iota(jnp.int32, (8, NB), 1)
    sub = lax.broadcasted_iota(jnp.int32, (8, NB), 0)
    done = []
    for base in range(0, NB, 8):
        top, rest = rest[:8], rest[8:]
        n = rest.shape[0]
        inside = (lane >= base) & (lane < base + 8)
        pivots = [jnp.broadcast_to(top[:, base + k : base + k + 1], (8, NB)) for k in range(8)]
        top = jnp.where(inside, jnp.where(lane - base == sub, 1.0, 0.0), top)
        if n:
            below = [jnp.broadcast_to(rest[:, base + k : base + k + 1], (n, NB)) for k in range(8)]
            wide = lax.broadcasted_iota(jnp.int32, (n, NB), 1)
            rest = jnp.where((wide >= base) & (wide < base + 8), 0.0, rest)
        for k in range(8):
            scale = lax.rsqrt(pivots[k][k : k + 1, :])
            row = top[k : k + 1, :] * scale
            factor = jnp.where(sub > k, pivots[k] * scale, 0.0)
            top = jnp.where(sub == k, row, top - factor * row)
            cross = {}
            for q in range(k + 1, 8):
                cross[q] = pivots[q][k : k + 1, :] * scale
                pivots[q] = pivots[q] - factor * cross[q]
            if n:
                lower = below[k] * scale
                rest = rest - lower * row
                for q in range(k + 1, 8):
                    below[q] = below[q] - lower * cross[q]
        done.append(top)
    return jnp.concatenate(done, axis=0)


def chol_steps(x, begin, end):
    r = lax.broadcasted_iota(jnp.int32, (NB, NB), 0)
    c = lax.broadcasted_iota(jnp.int32, (NB, NB), 1)

    def step(k, _):
        own = pl.ds(pl.multiple_of(k * NB, NB), NB)
        block = factor_block(x[own, own] + jnp.where(r == c, RIDGE, 0.0))
        x[own, own] = jnp.where(r == c, 1.0, 0.0)
        x[own, :] = dot(jnp.where(r >= c, block, 0.0), x[own, :], ((1,), (0,)))

        def trail(i, _):
            rows = pl.ds(pl.multiple_of(i * NB, NB), NB)
            factor = x[own, rows]
            x[rows, own] = jnp.zeros((NB, NB), jnp.float32)
            x[rows, :] = x[rows, :] - dot(factor, x[own, :], ((0,), (0,)))
            return 0

        lax.fori_loop(k + 1, N // NB, trail, 0)
        return 0

    lax.fori_loop(begin, end, step, 0)


def middle_kernel(
    gram, cross_half, left_panel,
    left_unit, right_panel, squares,
    x, slots, total, half_all, mate_half, own_squares, square_slots,
    z_send, z_recv, pair_send, pair_recv, col_send, col_recv,
):
    r, c, p = lax.axis_index("row"), lax.axis_index("col"), lax.axis_index("rep")
    mate = (r, c, 1 - p)
    barrier = pltpu.get_barrier_semaphore()
    pl.semaphore_signal(barrier, inc=1, device_id=mate, device_id_type=MESH)
    for step in range(1, 8):
        pl.semaphore_signal(barrier, inc=1, device_id=((r + step) % 8, c, p), device_id_type=MESH)
    for step in range(1, 16):
        pl.semaphore_signal(barrier, inc=1, device_id=(r, (c + step) % 16, p), device_id_type=MESH)
    pl.semaphore_wait(barrier, 23)

    started = []
    moves = []
    for step in range(1, 8):
        z = (r + step) % 8
        piece = cross_half.at[pl.ds(pl.multiple_of(32 * z, 32), 32)]
        move = remote(piece, slots.at[r], z_send.at[0, step], z_recv.at[0, step], (z, c, p))
        move.start()
        moves.append(move)
    slots[r] = cross_half[pl.ds(pl.multiple_of(32 * r, 32), 32), :]
    started += moves

    x[...] = gram[...]
    chol_steps(x, 0, 4)

    for move in moves:
        move.wait_recv()
    acc = slots[0]
    for z in range(1, 8):
        acc = acc + slots[z]
    total[...] = acc
    place = half_all.at[pl.ds(pl.multiple_of(32 * r, 32), 32)]
    place[...] = acc
    moves = []
    for step in range(1, 8):
        move = remote(total, place, z_send.at[1, step], z_recv.at[1, step], ((r + step) % 8, c, p))
        move.start()
        moves.append(move)
    started += moves

    chol_steps(x, 4, 7)

    for move in moves:
        move.wait_recv()
    swap = remote(half_all, mate_half, pair_send, pair_recv, mate)
    swap.start()
    started.append(swap)

    chol_steps(x, 7, 8)

    rows = lax.broadcasted_iota(jnp.int32, (256, 256), 0)
    cols = lax.broadcasted_iota(jnp.int32, (256, 256), 1)
    low = []
    for j in range(4):
        band = x[256 * j : 256 * j + 256, : 256 * j + 256]
        corner = jnp.where(rows >= cols, band[:, 256 * j :], 0.0)
        low.append(split(jnp.concatenate([band[:, : 256 * j], corner], axis=1) if j else corner))

    def solve(panel, out, at):
        high, rest = split(panel)
        for j in range(4):
            n = 256 * j + 256
            out[at, 256 * j : n] = dot3((high[:, :n], rest[:, :n]), low[j], ((1,), (1,)))

    swap.wait_recv()
    for q in range(2):
        @pl.when(p == q)
        def _():
            solve(half_all[...], right_panel, slice(256 * q, 256 * q + 256))
            solve(mate_half[...], right_panel, slice(256 - 256 * q, 512 - 256 * q))
    v = right_panel[...]
    sums = jnp.sum(v * v, axis=0, keepdims=True)
    for k in range(8):
        own_squares[k : k + 1, :] = sums[:, 128 * k : 128 * k + 128]
    square_slots[c] = own_squares[...]
    moves = []
    for step in range(1, 16):
        move = remote(own_squares, square_slots.at[c], col_send.at[step], col_recv.at[step], (r, (c + step) % 16, p))
        move.start()
        moves.append(move)
    started += moves
    solve(left_panel[...], left_unit, slice(0, 512))
    for move in moves:
        move.wait_recv()
    acc = square_slots[0]
    for i in range(1, 16):
        acc = acc + square_slots[i]
    for k in range(8):
        squares[:, 128 * k : 128 * k + 128] = acc[k : k + 1, :]
    for move in started:
        move.wait_send()


def middle(gram, cross_half, left_panel):
    f32 = jnp.float32
    vmem = pl.BlockSpec(memory_space=pltpu.VMEM)
    dma = pltpu.SemaphoreType.DMA
    return pl.pallas_call(
        middle_kernel,
        out_shape=[
            jax.ShapeDtypeStruct((512, N), f32),
            jax.ShapeDtypeStruct((512, N), f32),
            jax.ShapeDtypeStruct((1, N), f32),
        ],
        in_specs=[vmem] * 3,
        out_specs=[vmem] * 3,
        scratch_shapes=[
            pltpu.VMEM((N, N), f32),
            pltpu.VMEM((8, 32, N), f32),
            pltpu.VMEM((32, N), f32),
            pltpu.VMEM((256, N), f32),
            pltpu.VMEM((256, N), f32),
            pltpu.VMEM((8, 128), f32),
            pltpu.VMEM((16, 8, 128), f32),
            dma((2, 8)), dma((2, 8)), dma, dma, dma((16,)), dma((16,)),
        ],
        compiler_params=pltpu.CompilerParams(collective_id=1, has_side_effects=True, vmem_limit_bytes=50 << 20),
    )(gram, cross_half, left_panel)


def ring_scatter(piece, half, from_a, from_b, from_left, from_right, pos, left, right, send, recv, started):
    before, after, across = (pos + 3) % 4, (pos + 1) % 4, (pos + 2) % 4
    a = remote(half(across, 0), from_a, send.at[0], recv.at[0], left)
    b = remote(half(across, 1), from_b, send.at[1], recv.at[1], right)
    a.start()
    b.start()
    yield
    a.wait_recv()
    half(before, 0)[...] = half(before, 0)[...] + from_a[...]
    c = remote(piece(before), from_right, send.at[2], recv.at[2], left)
    c.start()
    b.wait_recv()
    half(after, 1)[...] = half(after, 1)[...] + from_b[...]
    d = remote(piece(after), from_left, send.at[3], recv.at[3], right)
    d.start()
    yield
    c.wait_recv()
    d.wait_recv()
    piece(pos)[...] = piece(pos)[...] + (from_left[...] + from_right[...])
    started += [a, b, c, d]


def ring_gather(piece, half, pos, left, right, send, recv, started, done=None):
    before, after, across = (pos + 3) % 4, (pos + 1) % 4, (pos + 2) % 4
    a = remote(piece(pos), piece(pos), send.at[0], recv.at[0], left)
    b = remote(piece(pos), piece(pos), send.at[1], recv.at[1], right)
    a.start()
    b.start()
    if done:
        done(0, pos)
    yield
    a.wait_recv()
    c = remote(half(after, 0), half(after, 0), send.at[2], recv.at[2], left)
    c.start()
    b.wait_recv()
    d = remote(half(before, 1), half(before, 1), send.at[3], recv.at[3], right)
    d.start()
    if done:
        done(1, after)
        done(2, before)
    yield
    c.wait_recv()
    d.wait_recv()
    if done:
        done(3, across)
    started += [a, b, c, d]


def lockstep(*stages):
    stages = list(stages)
    while stages:
        for stage in list(stages):
            try:
                next(stage)
            except StopIteration:
                stages.remove(stage)


def front_kernel(
    slab, momentum, basis,
    gram, buffer, left_panel, cross_half,
    part, total, landed, panel, from_a, from_b, from_left, from_right, from_a2, from_b2, from_left2, from_right2, full,
    gram_part, gram_in, gram_slots, gram_sum, gram_all, cross_part, cross_in,
    part_send, part_recv, land_send, land_recv, ring_send, ring_recv, z_send, z_recv, pair_send, pair_recv,
):
    r, c, p = lax.axis_index("row"), lax.axis_index("col"), lax.axis_index("rep")
    x, y = c // 4, c % 4
    mate = (r, c, 1 - p)
    sides = {
        "x": ((r, ((x + 3) % 4) * 4 + y, p), (r, ((x + 1) % 4) * 4 + y, p)),
        "y": ((r, x * 4 + (y + 3) % 4, p), (r, x * 4 + (y + 1) % 4, p)),
    }
    alone = (c // 8 == p) & (c % 2 == p)

    barrier = pltpu.get_barrier_semaphore()
    pl.semaphore_signal(barrier, inc=1, device_id=mate, device_id_type=MESH)
    for axis in ("x", "y"):
        for side in sides[axis]:
            pl.semaphore_signal(barrier, inc=1, device_id=side, device_id_type=MESH)
    for step in range(1, 8):
        pl.semaphore_signal(barrier, inc=1, device_id=((r + step) % 8, c, p), device_id_type=MESH)
    for slot in range(8):
        @pl.when(jnp.logical_not(alone & (8 * p + slot == c)))
        def _():
            pl.semaphore_signal(barrier, inc=1, device_id=(r, 8 * p + slot, c % 2), device_id_type=MESH)
    pl.semaphore_wait(barrier, jnp.where(alone, 19, 20))

    started = []

    first = c // 2
    copies = []
    for step in range(8):
        b = (first + step) % 8
        cols = pl.ds(pl.multiple_of(512 * (2 * b + 1 - p), 512), 512)
        copy = remote(slab.at[0, :, cols], part.at[step], part_send.at[step], part_recv.at[step], mate)
        copy.start()
        copies.append(copy)
    started += copies
    for step in range(8):
        b = (first + step) % 8
        d = 2 * b + p
        copies[step].wait_recv()
        cols = pl.ds(pl.multiple_of(512 * d, 512), 512)
        total[step] = part[step] + slab[0, :, cols]
        own = (d == c) & (c // 8 == p)

        @pl.when(own)
        def _():
            landed[c % 8] = total[step]

        @pl.when(jnp.logical_not(own))
        def _():
            remote(total.at[step], landed.at[c % 8], land_send.at[step], land_recv.at[c % 8], (r, d, c // 8)).start()

    for slot in range(8):
        @pl.when(jnp.logical_not(alone & (8 * p + slot == c)))
        def _():
            remote(total.at[0], landed.at[slot], land_send.at[0], land_recv.at[slot], (r, 8 * p + slot, c % 2)).wait_recv()
        buffer[64 * slot : 64 * slot + 64, :] = momentum[64 * slot : 64 * slot + 64, :] + landed[slot]

    across = {"x": (x + 2) % 4, "y": (y + 2) % 4}
    where = {"x": x, "y": y}

    def product(h):
        axis = "xy"[h]
        for t in range(4):
            if h == 0:
                rows = buffer[128 * t : 128 * t + 128, :]
            else:
                rows = jnp.concatenate([buffer[32 * (4 * u + t) : 32 * (4 * u + t) + 32, :] for u in range(4)], axis=0)
            got = dot(rows, basis[:, 512 * h : 512 * h + 512], ((1,), (0,)))
            for u in range(4):
                panel[h, t, u] = got[32 * u : 32 * u + 32]

    def scatter(h):
        axis, other = ("x", "y") if h == 0 else ("y", "x")
        product(h)
        yield from ring_scatter(
            lambda i: panel.at[h, i],
            lambda i, k: panel.at[h, i, pl.ds(2 * k, 2)],
            from_a.at[h], from_b.at[h], from_left.at[h], from_right.at[h],
            where[axis], *sides[axis], ring_send.at[h, 0], ring_recv.at[h, 0], started,
        )
        yield
        yield from ring_scatter(
            lambda i: panel.at[h, where[axis], i],
            lambda i, k: panel.at[h, where[axis], i, pl.ds(16 * k, 16)],
            from_a2.at[h], from_b2.at[h], from_left2.at[h], from_right2.at[h],
            where[other], *sides[other], ring_send.at[h, 1], ring_recv.at[h, 1], started,
        )
        full[h, where[axis], where[other]] = panel[h, where[axis], where[other]]
        yield
        yield from ring_gather(
            lambda i: full.at[h, where[axis], i],
            lambda i, k: full.at[h, where[axis], i, pl.ds(16 * k, 16)],
            where[other], *sides[other], ring_send.at[h, 2], ring_recv.at[h, 2], started,
        )
        yield
        yield from ring_gather(
            lambda i: full.at[h, i],
            lambda i, k: full.at[h, i, pl.ds(2 * k, 2)],
            where[axis], *sides[axis], ring_send.at[h, 3], ring_recv.at[h, 3], started,
        )

    lockstep(scatter(0), scatter(1))
    for u in range(4):
        for v in range(4):
            rows = slice(32 * (4 * u + v), 32 * (4 * u + v) + 32)
            left_panel[rows, 0:512] = full[0, u, v]
            left_panel[rows, 512:1024] = full[1, v, u]

    rows = pl.ds(pl.multiple_of(128 * (c // 2), 128), 128)
    mine = left_panel[:, rows]
    for q in range(2):
        cols = pl.ds(pl.multiple_of(512 * (c % 2) + 256 * q, 256), 256)
        gram_part[q] = dot(mine, left_panel[:, cols], ((0,), (0,)))
    swap = remote(gram_part.at[1 - p], gram_in, pair_send.at[8], pair_recv.at[8], mate)
    swap.start()
    started.append(swap)

    for q in range(2):
        cross_part[q] = dot(buffer[:, 256 * q : 256 * q + 256], left_panel[...], ((0,), (0,)))
    cross_swap = remote(cross_part.at[1 - p], cross_in, pair_send.at[9], pair_recv.at[9], mate)
    cross_swap.start()
    started.append(cross_swap)

    swap.wait_recv()
    gram_part[p] = gram_part[p] + gram_in[...]
    moves = []
    for step in range(1, 8):
        z = (r + step) % 8
        piece = gram_part.at[p, pl.ds(pl.multiple_of(16 * z, 16), 16)]
        move = remote(piece, gram_slots.at[r], z_send.at[0, step], z_recv.at[0, step], (z, c, p))
        move.start()
        moves.append(move)
    gram_slots[r] = gram_part[p, pl.ds(pl.multiple_of(16 * r, 16), 16)]
    started += moves
    for move in moves:
        move.wait_recv()
    acc = gram_slots[0]
    for z in range(1, 8):
        acc = acc + gram_slots[z]
    h = r // 4
    f, s = jnp.where(h == 0, x, y), jnp.where(h == 0, y, x)
    place = gram_all.at[p, h, f, s, pl.ds(pl.multiple_of(16 * (r % 4), 16), 16)]
    gram_sum[...] = acc
    place[...] = acc
    moves = []
    for step in range(1, 8):
        move = remote(gram_sum, place, z_send.at[1, step], z_recv.at[1, step], ((r + step) % 8, c, p))
        move.start()
        moves.append(move)
    started += moves
    for move in moves:
        move.wait_recv()

    pairs = []

    def gather(h):
        axis, other = ("x", "y") if h == 0 else ("y", "x")
        yield from ring_gather(
            lambda i: gram_all.at[p, h, where[axis], i],
            lambda i, k: gram_all.at[p, h, where[axis], i, pl.ds(32 * k, 32)],
            where[other], *sides[other], ring_send.at[h, 4], ring_recv.at[h, 4], started,
        )
        yield

        def forward(k, i):
            view = gram_all.at[p, h, i]
            copy = remote(view, view, pair_send.at[4 * h + k], pair_recv.at[4 * h + k], mate)
            copy.start()
            pairs.append(copy)

        yield from ring_gather(
            lambda i: gram_all.at[p, h, i],
            lambda i, k: gram_all.at[p, h, i, pl.ds(2 * k, 2)],
            where[axis], *sides[axis], ring_send.at[h, 5], ring_recv.at[h, 5], started, forward,
        )

    lockstep(gather(0), gather(1))
    for copy in pairs:
        copy.wait_recv()
    started += pairs
    for q in range(2):
        for u in range(4):
            for v in range(4):
                n = 4 * u + v
                cols = slice(512 * (n % 2) + 256 * q, 512 * (n % 2) + 256 * q + 256)
                top = 128 * (n // 2)
                gram[top : top + 64, cols] = gram_all[q, 0, u, v]
                gram[top + 64 : top + 128, cols] = gram_all[q, 1, v, u]

    cross_swap.wait_recv()
    cross_half[...] = cross_part[p] + cross_in[...]
    for copy in started:
        copy.wait_send()
    for step in range(8):
        b = (first + step) % 8
        d = 2 * b + p

        @pl.when(jnp.logical_not((d == c) & (c // 8 == p)))
        def _():
            remote(total.at[step], landed.at[c % 8], land_send.at[step], land_recv.at[c % 8], (r, d, c // 8)).wait_send()


def front(gradients, momentum, right_basis):
    f32 = jnp.float32
    vmem = pl.BlockSpec(memory_space=pltpu.VMEM)
    dma = pltpu.SemaphoreType.DMA
    return pl.pallas_call(
        front_kernel,
        out_shape=[
            jax.ShapeDtypeStruct((N, N), f32),
            jax.ShapeDtypeStruct((512, 512), f32),
            jax.ShapeDtypeStruct((512, N), f32),
            jax.ShapeDtypeStruct((256, N), f32),
        ],
        in_specs=[vmem] * 3,
        out_specs=[vmem] * 4,
        scratch_shapes=[
            pltpu.VMEM((8, 64, 512), f32),
            pltpu.VMEM((8, 64, 512), f32),
            pltpu.VMEM((8, 64, 512), f32),
            pltpu.VMEM((2, 4, 4, 32, 512), f32),
            pltpu.VMEM((2, 2, 32, 512), f32),
            pltpu.VMEM((2, 2, 32, 512), f32),
            pltpu.VMEM((2, 4, 32, 512), f32),
            pltpu.VMEM((2, 4, 32, 512), f32),
            pltpu.VMEM((2, 16, 512), f32),
            pltpu.VMEM((2, 16, 512), f32),
            pltpu.VMEM((2, 32, 512), f32),
            pltpu.VMEM((2, 32, 512), f32),
            pltpu.VMEM((2, 4, 4, 32, 512), f32),
            pltpu.VMEM((2, 128, 256), f32),
            pltpu.VMEM((128, 256), f32),
            pltpu.VMEM((8, 16, 256), f32),
            pltpu.VMEM((16, 256), f32),
            pltpu.VMEM((2, 2, 4, 4, 64, 256), f32),
            pltpu.VMEM((2, 256, N), f32),
            pltpu.VMEM((256, N), f32),
            dma((8,)), dma((8,)), dma((8,)), dma((8,)),
            dma((2, 6, 4)), dma((2, 6, 4)),
            dma((2, 8)), dma((2, 8)),
            dma((10,)), dma((10,)),
        ],
        compiler_params=pltpu.CompilerParams(
            collective_id=0, has_side_effects=True, vmem_limit_bytes=50 << 20
        ),
    )(gradients, momentum, right_basis)


def shards(gradients, momentum, right_basis):
    gram, buffer, left_panel, cross_half = front(gradients, momentum, right_basis)
    left_unit, right_panel, squares = middle(gram, cross_half, left_panel)
    new_basis = right_panel / jnp.sqrt(squares + EPSILON)
    fine = lax.Precision.HIGH
    new_momentum = buffer - (1.0 - DECAY) * dot(left_unit, right_panel, ((1,), (1,)), fine)
    update = (D / math.sqrt(N)) * dot(left_unit, new_basis, ((1,), (1,)), fine)
    return (new_momentum, new_basis, update)


def solution(mesh):
    return jax.shard_map(
        shards,
        mesh=mesh,
        in_specs=(P("rep", ("row", "col"), None), P(("row", "rep"), "col"), P("col", None)),
        out_specs=(P(("row", "rep"), "col"), P("col", None), P(("row", "rep"), "col")),
        check_vma=False,
    )
```

```python
import functools
import math

import jax
import jax.numpy as jnp
from jax import lax
from jax.experimental import pallas as pl
from jax.experimental.pallas import tpu as pltpu
from jax.sharding import PartitionSpec as P

N = 1024
NB = 128
HI = lax.Precision.HIGHEST
EPSILON = 1e-06
RIDGE = 0.001
DECAY = 0.95
D = 8192
MESH = pl.DeviceIdType.MESH


def dot(left, right, dims, precision=HI):
    return lax.dot_general(left, right, (dims, ((), ())), precision=precision, preferred_element_type=jnp.float32)


def split(a):
    high = a.astype(jnp.bfloat16)
    return high, (a - high.astype(jnp.float32)).astype(jnp.bfloat16)


def dot3(left, right, dims):
    def one(a, b):
        return lax.dot_general(a, b, (dims, ((), ())), preferred_element_type=jnp.float32)

    return one(left[0], right[0]) + (one(left[0], right[1]) + one(left[1], right[0]))


def factor_block(rest):
    lane = lax.broadcasted_iota(jnp.int32, (8, NB), 1)
    sub = lax.broadcasted_iota(jnp.int32, (8, NB), 0)
    done = []
    for base in range(0, NB, 8):
        top, rest = rest[:8], rest[8:]
        n = rest.shape[0]
        inside = (lane >= base) & (lane < base + 8)
        pivots = [jnp.broadcast_to(top[:, base + k : base + k + 1], (8, NB)) for k in range(8)]
        top = jnp.where(inside, jnp.where(lane - base == sub, 1.0, 0.0), top)
        if n:
            below = [jnp.broadcast_to(rest[:, base + k : base + k + 1], (n, NB)) for k in range(8)]
            wide = lax.broadcasted_iota(jnp.int32, (n, NB), 1)
            rest = jnp.where((wide >= base) & (wide < base + 8), 0.0, rest)
        for k in range(8):
            scale = lax.rsqrt(pivots[k][k : k + 1, :])
            row = top[k : k + 1, :] * scale
            factor = jnp.where(sub > k, pivots[k] * scale, 0.0)
            top = jnp.where(sub == k, row, top - factor * row)
            cross = {}
            for q in range(k + 1, 8):
                cross[q] = pivots[q][k : k + 1, :] * scale
                pivots[q] = pivots[q] - factor * cross[q]
            if n:
                lower = below[k] * scale
                rest = rest - lower * row
                for q in range(k + 1, 8):
                    below[q] = below[q] - lower * cross[q]
        done.append(top)
    return jnp.concatenate(done, axis=0)


def remote(src, dst, send, recv, device):
    return pltpu.make_async_remote_copy(
        src_ref=src, dst_ref=dst, send_sem=send, recv_sem=recv, device_id=device, device_id_type=MESH
    )


def ring_scatter(piece, half, from_a, from_b, from_left, from_right, pos, left, right, send, recv, started):
    before, after, across = (pos + 3) % 4, (pos + 1) % 4, (pos + 2) % 4
    a = remote(half(across, 0), from_a, send.at[0], recv.at[0], left)
    b = remote(half(across, 1), from_b, send.at[1], recv.at[1], right)
    a.start()
    b.start()
    yield
    a.wait_recv()
    half(before, 0)[...] = half(before, 0)[...] + from_a[...]
    c = remote(piece(before), from_right, send.at[2], recv.at[2], left)
    c.start()
    b.wait_recv()
    half(after, 1)[...] = half(after, 1)[...] + from_b[...]
    d = remote(piece(after), from_left, send.at[3], recv.at[3], right)
    d.start()
    yield
    c.wait_recv()
    d.wait_recv()
    piece(pos)[...] = piece(pos)[...] + (from_left[...] + from_right[...])
    started += [a, b, c, d]


def ring_gather(piece, half, pos, left, right, send, recv, started, done=None):
    before, after, across = (pos + 3) % 4, (pos + 1) % 4, (pos + 2) % 4
    a = remote(piece(pos), piece(pos), send.at[0], recv.at[0], left)
    b = remote(piece(pos), piece(pos), send.at[1], recv.at[1], right)
    a.start()
    b.start()
    if done:
        done(0, pos)
    yield
    a.wait_recv()
    c = remote(half(after, 0), half(after, 0), send.at[2], recv.at[2], left)
    c.start()
    b.wait_recv()
    d = remote(half(before, 1), half(before, 1), send.at[3], recv.at[3], right)
    d.start()
    if done:
        done(1, after)
        done(2, before)
    yield
    c.wait_recv()
    d.wait_recv()
    if done:
        done(3, across)
    started += [a, b, c, d]


def lockstep(*stages):
    stages = list(stages)
    while stages:
        for stage in list(stages):
            try:
                next(stage)
            except StopIteration:
                stages.remove(stage)


def place_rows(x, gram_all, k):
    rows = slice(NB * k, NB * k + NB)
    for j in range(k, N // NB):
        parts = [gram_all[p, k, 2 * j + h] for h in range(2) for p in range(2)]
        block = jnp.concatenate(parts, axis=0)
        cols = slice(NB * j, NB * j + NB)
        x[rows, cols] = block if k == 0 else x[rows, cols] + block


def chol_step(x, k):
    r = lax.broadcasted_iota(jnp.int32, (NB, NB), 0)
    c = lax.broadcasted_iota(jnp.int32, (NB, NB), 1)
    a, b = NB * k, NB * k + NB
    block = factor_block(x[a:b, a:b] + jnp.where(r == c, RIDGE, 0.0))
    low = jnp.where(r >= c, block, 0.0)
    x[a:b, a:b] = low
    if a:
        x[a:b, :a] = dot(low, x[a:b, :a], ((1,), (0,)))
    if b < N:
        x[a:b, b:] = dot(low, x[a:b, b:], ((1,), (0,)))
    for i in range(b, N, NB):
        factor = x[a:b, i : i + NB]
        left = dot(factor, x[a:b, :b], ((0,), (0,)))
        right = dot(factor, x[a:b, i:], ((0,), (0,)))
        x[i : i + NB, a:b] = -left[:, a:]
        if a:
            x[i : i + NB, :a] = x[i : i + NB, :a] - left[:, :a]
            x[i : i + NB, i:] = x[i : i + NB, i:] - right
        else:
            x[i : i + NB, i:] = -right


def main_kernel(
    slab, momentum, basis,
    buffer, left_unit, right_panel, squares,
    part, total, landed, basis_high, basis_low, panel, from_a, from_b, from_left, from_right,
    from_a2, from_b2, from_left2, from_right2, full, left_panel,
    gram_part, gram_pieces, gram_in, gram_slots, gram_all, x,
    cross_part, cross_in, slots, half_all, mate_half, own_squares, square_slots,
    part_send, part_recv, land_send, land_recv, ring_send, ring_recv, z_send, z_recv,
    pair_send, pair_recv, chunk_send, chunk_recv, pass_send, pass_recv, col_send, col_recv,
):
    r, c, p = lax.axis_index("row"), lax.axis_index("col"), lax.axis_index("rep")
    x_at, y_at = c // 4, c % 4
    mate = (r, c, 1 - p)
    sides = {
        "x": ((r, ((x_at + 3) % 4) * 4 + y_at, p), (r, ((x_at + 1) % 4) * 4 + y_at, p)),
        "y": ((r, x_at * 4 + (y_at + 3) % 4, p), (r, x_at * 4 + (y_at + 1) % 4, p)),
    }
    where = {"x": x_at, "y": y_at}
    alone = (c // 8 == p) & (c % 2 == p)

    def peer(step):
        return (r, (c + step) % 16, p)

    def level(step):
        return ((r + step) % 8, c, p)

    barrier = pltpu.get_barrier_semaphore()
    pl.semaphore_signal(barrier, inc=1, device_id=mate, device_id_type=MESH)
    for step in range(1, 16):
        pl.semaphore_signal(barrier, inc=1, device_id=peer(step), device_id_type=MESH)
    for step in range(1, 8):
        pl.semaphore_signal(barrier, inc=1, device_id=level(step), device_id_type=MESH)
    for slot in range(8):
        @pl.when(jnp.logical_not(alone & (8 * p + slot == c)))
        def _():
            pl.semaphore_signal(barrier, inc=1, device_id=(r, 8 * p + slot, c % 2), device_id_type=MESH)
    pl.semaphore_wait(barrier, jnp.where(alone, 30, 31))

    started = []

    first = c // 2
    copies = {}
    for q in range(2):
        for step in range(8):
            b = (first + step) % 8
            cols = pl.ds(pl.multiple_of(512 * (2 * b + 1 - p), 512), 512)
            copy = remote(
                slab.at[0, pl.ds(32 * q, 32), cols], part.at[q, step], part_send.at[q, step], part_recv.at[q, step], mate
            )
            copy.start()
            copies[q, step] = copy
            started.append(copy)

    def block_copy(q, step):
        d = 2 * ((first + step) % 8) + p
        own = (d == c) & (c // 8 == p)
        slot = c % 8
        return own, remote(
            total.at[q, step], landed.at[q, slot], land_send.at[q, step], land_recv.at[q, slot], (r, d, c // 8)
        )

    for q in range(2):
        for step in range(8):
            copies[q, step].wait_recv()
            cols = pl.ds(pl.multiple_of(512 * (2 * ((first + step) % 8) + p), 512), 512)
            total[q, step] = part[q, step] + slab[0, 32 * q : 32 * q + 32, cols]
            own, copy = block_copy(q, step)

            @pl.when(own)
            def _():
                landed[q, c % 8] = total[q, step]

            @pl.when(jnp.logical_not(own))
            def _():
                copy.start()

    high, low = split(basis[...])
    basis_high[...] = high
    basis_low[...] = low

    def land(q):
        for slot in range(8):
            @pl.when(jnp.logical_not(alone & (8 * p + slot == c)))
            def _():
                remote(
                    total.at[q, 0], landed.at[q, slot], land_send.at[q, 0], land_recv.at[q, slot],
                    (r, 8 * p + slot, c % 2),
                ).wait_recv()
            rows = slice(64 * slot + 32 * q, 64 * slot + 32 * q + 32)
            buffer[rows, :] = momentum[rows, :] + landed[q, slot]
        tile = jnp.concatenate([buffer[64 * s + 32 * q : 64 * s + 32 * q + 32, :] for s in range(8)], axis=0)
        tile = split(tile)
        for h in range(2):
            cols = slice(512 * h, 512 * h + 512)
            got = dot3(tile, (basis_high[:, cols], basis_low[:, cols]), ((1,), (0,)))
            for u in range(4):
                for v in range(4):
                    n = 4 * u + v
                    f, s = (u, v) if h == 0 else (v, u)
                    panel[q, h, f, s] = got[16 * n : 16 * n + 16]

    def total_over_col(q, h):
        axis, other = ("x", "y") if h == 0 else ("y", "x")
        f, s = where[axis], where[other]
        yield from ring_scatter(
            lambda i: panel.at[q, h, i],
            lambda i, k: panel.at[q, h, i, pl.ds(2 * k, 2)],
            from_a.at[q, h], from_b.at[q, h], from_left.at[q, h], from_right.at[q, h],
            f, *sides[axis], ring_send.at[q, h, 0], ring_recv.at[q, h, 0], started,
        )
        yield from ring_scatter(
            lambda i: panel.at[q, h, f, i],
            lambda i, k: panel.at[q, h, f, i, pl.ds(8 * k, 8)],
            from_a2.at[q, h], from_b2.at[q, h], from_left2.at[q, h], from_right2.at[q, h],
            s, *sides[other], ring_send.at[q, h, 1], ring_recv.at[q, h, 1], started,
        )
        full[q, h, f, s] = panel[q, h, f, s]
        yield from ring_gather(
            lambda i: full.at[q, h, f, i],
            lambda i, k: full.at[q, h, f, i, pl.ds(8 * k, 8)],
            s, *sides[other], ring_send.at[q, h, 2], ring_recv.at[q, h, 2], started,
        )
        yield from ring_gather(
            lambda i: full.at[q, h, i],
            lambda i, k: full.at[q, h, i, pl.ds(2 * k, 2)],
            f, *sides[axis], ring_send.at[q, h, 3], ring_recv.at[q, h, 3], started,
        )

    sums = {(q, h): total_over_col(q, h) for q in range(2) for h in range(2)}
    for q in range(2):
        land(q)
        for h in range(2):
            next(sums[q, h])
    lockstep(sums[0, 0], sums[0, 1], sums[1, 0], sums[1, 1])
    for q in range(2):
        for u in range(4):
            for v in range(4):
                n = 4 * u + v
                top = 64 * (n // 2) + 32 * q + 16 * (n % 2)
                left_panel[top : top + 16, 0:512] = full[q, 0, u, v]
                left_panel[top : top + 16, 512:1024] = full[q, 1, v, u]

    column = pl.ds(pl.multiple_of(NB * (c // 2), NB), NB)
    left_split = split(left_panel[...])
    gram_part[...] = dot3(left_split, split(left_panel[:, column]), ((0,), (0,)))
    for q in range(2):
        for b in range(8):
            rows = pl.ds(pl.multiple_of(NB * b + 64 * (c % 2) + 32 * q, 32), 32)
            gram_pieces[q, b] = gram_part[rows, :]
    swap = remote(gram_pieces.at[1 - p], gram_in, pair_send.at[0], pair_recv.at[0], mate)
    swap.start()
    started.append(swap)

    def cross(q):
        cross_part[q] = dot3(split(buffer[:, 256 * q : 256 * q + 256]), left_split, ((0,), (0,)))

    swap.wait_recv()
    gram_pieces[p] = gram_pieces[p] + gram_in[...]
    moves = []
    for step in range(1, 8):
        z = (r + step) % 8
        move = remote(gram_pieces.at[p, z], gram_slots.at[r], z_send.at[0, step], z_recv.at[0, step], level(step))
        move.start()
        moves.append(move)
    started += moves
    gram_slots[r] = gram_pieces[p, r]
    cross(0)
    for move in moves:
        move.wait_recv()
    acc = gram_slots[0]
    for z in range(1, 8):
        acc = acc + gram_slots[z]
    gram_all[p, r, c] = acc
    moves = []
    for step in range(1, 8):
        own = gram_all.at[p, r, c]
        move = remote(own, own, z_send.at[1, step], z_recv.at[1, step], level(step))
        move.start()
        moves.append(move)
    started += moves
    cross(1)
    cross_swap = remote(cross_part.at[1 - p], cross_in, pair_send.at[1], pair_recv.at[1], mate)
    cross_swap.start()
    started.append(cross_swap)
    for move in moves:
        move.wait_recv()

    def chunk_copy(b, step):
        own = gram_all.at[p, b, c]
        return remote(own, own, chunk_send.at[b, step], chunk_recv.at[b, step], peer(step))

    def chunk_start(b):
        @pl.when(c // 2 >= b)
        def _():
            for step in range(1, 16):
                chunk_copy(b, step).start()

    passed = {}

    def chunk_pass(b):
        for step in range(1, 16):
            @pl.when(((c + 16 - step) % 16) // 2 >= b)
            def _():
                chunk_copy(b, step).wait_recv()
        view = gram_all.at[p, b, pl.ds(2 * b, 16 - 2 * b)]
        passed[b] = remote(view, view, pass_send.at[b], pass_recv.at[b], mate)
        passed[b].start()
        started.append(passed[b])

    def rows_of(z):
        return pl.ds(pl.multiple_of(32 * z, 32), 32)

    chunk_start(0)
    chunk_start(1)
    chunk_pass(0)
    moves = []
    handed = {}

    def hand(step):
        view = half_all.at[rows_of((r + 8 - step) % 8)]
        into = mate_half.at[rows_of((r + 8 - step) % 8)]
        handed[step] = remote(view, into, pass_send.at[8 + step], pass_recv.at[8 + step], mate)
        handed[step].start()
        started.append(handed[step])

    for k in range(8):
        passed[k].wait_recv()
        if k + 1 < 8:
            chunk_pass(k + 1)
        if k + 2 < 8:
            chunk_start(k + 2)
        if k == 0:
            cross_swap.wait_recv()
            cross_part[p] = cross_part[p] + cross_in[...]
            for step in range(1, 8):
                z = (r + step) % 8
                move = remote(cross_part.at[p, rows_of(z)], slots.at[r], z_send.at[2, step], z_recv.at[2, step], level(step))
                move.start()
                moves.append(move)
            started += moves
            slots[r] = cross_part[p, rows_of(r), :]
        if k == 4:
            for move in moves:
                move.wait_recv()
            acc = slots[0]
            for z in range(1, 8):
                acc = acc + slots[z]
            own_rows = half_all.at[rows_of(r)]
            own_rows[...] = acc
            moves = []
            for step in range(1, 8):
                move = remote(own_rows, own_rows, z_send.at[3, step], z_recv.at[3, step], level(step))
                move.start()
                moves.append(move)
            started += moves
            hand(0)
        if k == 7:
            for step in (1, 7, 2, 6):
                moves[step - 1].wait_recv()
                hand(step)
        place_rows(x, gram_all, k)
        chol_step(x, k)

    for step in (3, 5, 4):
        moves[step - 1].wait_recv()
        hand(step)

    rows = lax.broadcasted_iota(jnp.int32, (256, 256), 0)
    cols = lax.broadcasted_iota(jnp.int32, (256, 256), 1)
    bands = []
    for j in range(4):
        band = x[256 * j : 256 * j + 256, : 256 * j + 256]
        corner = jnp.where(rows >= cols, band[:, 256 * j :], 0.0)
        bands.append(split(jnp.concatenate([band[:, : 256 * j], corner], axis=1) if j else corner))

    def solve(panel_split, out, at):
        for j in range(4):
            n = 256 * j + 256
            out[at, 256 * j : n] = dot3((panel_split[0][:, :n], panel_split[1][:, :n]), bands[j], ((1,), (1,)))

    for step in range(8):
        handed[step].wait_recv()
    for q in range(2):
        @pl.when(p == q)
        def _():
            solve(split(half_all[...]), right_panel, slice(256 * q, 256 * q + 256))
            solve(split(mate_half[...]), right_panel, slice(256 - 256 * q, 512 - 256 * q))
    v = right_panel[...]
    square_sums = jnp.sum(v * v, axis=0, keepdims=True)
    for k in range(8):
        own_squares[k : k + 1, :] = square_sums[:, 128 * k : 128 * k + 128]
    square_slots[c] = own_squares[...]
    moves = []
    for step in range(1, 16):
        move = remote(own_squares, square_slots.at[c], col_send.at[step], col_recv.at[step], peer(step))
        move.start()
        moves.append(move)
    started += moves
    solve(split(left_panel[...]), left_unit, slice(0, 512))
    for move in moves:
        move.wait_recv()
    acc = square_slots[0]
    for i in range(1, 16):
        acc = acc + square_slots[i]
    for k in range(8):
        squares[:, 128 * k : 128 * k + 128] = acc[k : k + 1, :]

    for move in started:
        move.wait_send()
    for q in range(2):
        for step in range(8):
            own, copy = block_copy(q, step)

            @pl.when(jnp.logical_not(own))
            def _():
                copy.wait_send()
    for b in range(8):
        @pl.when(c // 2 >= b)
        def _():
            for step in range(1, 16):
                chunk_copy(b, step).wait_send()


def panels(gradients, momentum, right_basis):
    f32 = jnp.float32
    vmem = pl.BlockSpec(memory_space=pltpu.VMEM)
    dma = pltpu.SemaphoreType.DMA
    return pl.pallas_call(
        main_kernel,
        out_shape=[
            jax.ShapeDtypeStruct((512, 512), f32),
            jax.ShapeDtypeStruct((512, N), f32),
            jax.ShapeDtypeStruct((512, N), f32),
            jax.ShapeDtypeStruct((1, N), f32),
        ],
        in_specs=[vmem] * 3,
        out_specs=[vmem] * 4,
        scratch_shapes=[
            pltpu.VMEM((2, 8, 32, 512), f32),
            pltpu.VMEM((2, 8, 32, 512), f32),
            pltpu.VMEM((2, 8, 32, 512), f32),
            pltpu.VMEM((512, N), jnp.bfloat16),
            pltpu.VMEM((512, N), jnp.bfloat16),
            pltpu.VMEM((2, 2, 4, 4, 16, 512), f32),
            pltpu.VMEM((2, 2, 2, 16, 512), f32),
            pltpu.VMEM((2, 2, 2, 16, 512), f32),
            pltpu.VMEM((2, 2, 4, 16, 512), f32),
            pltpu.VMEM((2, 2, 4, 16, 512), f32),
            pltpu.VMEM((2, 2, 8, 512), f32),
            pltpu.VMEM((2, 2, 8, 512), f32),
            pltpu.VMEM((2, 2, 16, 512), f32),
            pltpu.VMEM((2, 2, 16, 512), f32),
            pltpu.VMEM((2, 2, 4, 4, 16, 512), f32),
            pltpu.VMEM((512, N), f32),
            pltpu.VMEM((N, NB), f32),
            pltpu.VMEM((2, 8, 32, NB), f32),
            pltpu.VMEM((8, 32, NB), f32),
            pltpu.VMEM((8, 32, NB), f32),
            pltpu.VMEM((2, 8, 16, 32, NB), f32),
            pltpu.VMEM((N, N), f32),
            pltpu.VMEM((2, 256, N), f32),
            pltpu.VMEM((256, N), f32),
            pltpu.VMEM((8, 32, N), f32),
            pltpu.VMEM((256, N), f32),
            pltpu.VMEM((256, N), f32),
            pltpu.VMEM((8, 128), f32),
            pltpu.VMEM((16, 8, 128), f32),
            dma((2, 8)), dma((2, 8)), dma((2, 8)), dma((2, 8)),
            dma((2, 2, 4, 4)), dma((2, 2, 4, 4)),
            dma((4, 8)), dma((4, 8)),
            dma((2,)), dma((2,)),
            dma((8, 16)), dma((8, 16)),
            dma((16,)), dma((16,)),
            dma((16,)), dma((16,)),
        ],
        compiler_params=pltpu.CompilerParams(collective_id=0, has_side_effects=True, vmem_limit_bytes=56 << 20),
    )(gradients, momentum, right_basis)


def shards(gradients, momentum, right_basis):
    buffer, left_unit, right_panel, squares = panels(gradients, momentum, right_basis)
    new_basis = right_panel / jnp.sqrt(squares + EPSILON)
    fine = lax.Precision.HIGH
    new_momentum = buffer - (1.0 - DECAY) * dot(left_unit, right_panel, ((1,), (1,)), fine)
    update = (D / math.sqrt(N)) * dot(left_unit, new_basis, ((1,), (1,)), fine)
    return (new_momentum, new_basis, update)


def solution(mesh):
    return jax.shard_map(
        shards,
        mesh=mesh,
        in_specs=(P("rep", ("row", "col"), None), P(("row", "rep"), "col"), P("col", None)),
        out_specs=(P(("row", "rep"), "col"), P("col", None), P(("row", "rep"), "col")),
        check_vma=False,
    )
```

```python
import functools
import math

import jax
import jax.numpy as jnp
from jax import lax
from jax.experimental import pallas as pl
from jax.experimental.pallas import tpu as pltpu
from jax.sharding import PartitionSpec as P

N = 1024
NB = 128
HI = lax.Precision.HIGHEST
EPSILON = 1e-06
RIDGE = 0.001
DECAY = 0.95
D = 8192
MESH = pl.DeviceIdType.MESH


def dot(left, right, dims, precision=HI):
    return lax.dot_general(left, right, (dims, ((), ())), precision=precision, preferred_element_type=jnp.float32)


def split(a):
    high = a.astype(jnp.bfloat16)
    return high, (a - high.astype(jnp.float32)).astype(jnp.bfloat16)


def dot3(left, right, dims):
    def one(a, b):
        return lax.dot_general(a, b, (dims, ((), ())), preferred_element_type=jnp.float32)

    return one(left[0], right[0]) + (one(left[0], right[1]) + one(left[1], right[0]))


def factor_block(rest):
    lane = lax.broadcasted_iota(jnp.int32, (8, NB), 1)
    sub = lax.broadcasted_iota(jnp.int32, (8, NB), 0)
    done = []
    for base in range(0, NB, 8):
        top, rest = rest[:8], rest[8:]
        n = rest.shape[0]
        inside = (lane >= base) & (lane < base + 8)
        pivots = [jnp.broadcast_to(top[:, base + k : base + k + 1], (8, NB)) for k in range(8)]
        top = jnp.where(inside, jnp.where(lane - base == sub, 1.0, 0.0), top)
        if n:
            below = [jnp.broadcast_to(rest[:, base + k : base + k + 1], (n, NB)) for k in range(8)]
            wide = lax.broadcasted_iota(jnp.int32, (n, NB), 1)
            rest = jnp.where((wide >= base) & (wide < base + 8), 0.0, rest)
        for k in range(8):
            scale = lax.rsqrt(pivots[k][k : k + 1, :])
            row = top[k : k + 1, :] * scale
            factor = jnp.where(sub > k, pivots[k] * scale, 0.0)
            top = jnp.where(sub == k, row, top - factor * row)
            cross = {}
            for q in range(k + 1, 8):
                cross[q] = pivots[q][k : k + 1, :] * scale
                pivots[q] = pivots[q] - factor * cross[q]
            if n:
                lower = below[k] * scale
                rest = rest - lower * row
                for q in range(k + 1, 8):
                    below[q] = below[q] - lower * cross[q]
        done.append(top)
    return jnp.concatenate(done, axis=0)


def remote(src, dst, send, recv, device):
    return pltpu.make_async_remote_copy(
        src_ref=src, dst_ref=dst, send_sem=send, recv_sem=recv, device_id=device, device_id_type=MESH
    )


def ring_scatter(piece, half, from_a, from_b, from_left, from_right, pos, left, right, send, recv, started):
    before, after, across = (pos + 3) % 4, (pos + 1) % 4, (pos + 2) % 4
    a = remote(half(across, 0), from_a, send.at[0], recv.at[0], left)
    b = remote(half(across, 1), from_b, send.at[1], recv.at[1], right)
    a.start()
    b.start()
    yield
    a.wait_recv()
    half(before, 0)[...] = half(before, 0)[...] + from_a[...]
    c = remote(piece(before), from_right, send.at[2], recv.at[2], left)
    c.start()
    b.wait_recv()
    half(after, 1)[...] = half(after, 1)[...] + from_b[...]
    d = remote(piece(after), from_left, send.at[3], recv.at[3], right)
    d.start()
    yield
    c.wait_recv()
    d.wait_recv()
    piece(pos)[...] = piece(pos)[...] + (from_left[...] + from_right[...])
    started += [a, b, c, d]


def ring_gather(piece, half, pos, left, right, send, recv, started, done=None):
    before, after, across = (pos + 3) % 4, (pos + 1) % 4, (pos + 2) % 4
    a = remote(piece(pos), piece(pos), send.at[0], recv.at[0], left)
    b = remote(piece(pos), piece(pos), send.at[1], recv.at[1], right)
    a.start()
    b.start()
    if done:
        done(0, pos)
    yield
    a.wait_recv()
    c = remote(half(after, 0), half(after, 0), send.at[2], recv.at[2], left)
    c.start()
    b.wait_recv()
    d = remote(half(before, 1), half(before, 1), send.at[3], recv.at[3], right)
    d.start()
    if done:
        done(1, after)
        done(2, before)
    yield
    c.wait_recv()
    d.wait_recv()
    if done:
        done(3, across)
    started += [a, b, c, d]


def lockstep(*stages):
    stages = list(stages)
    while stages:
        for stage in list(stages):
            try:
                next(stage)
            except StopIteration:
                stages.remove(stage)


def place_rows(x, gram_all, k):
    rows = slice(NB * k, NB * k + NB)
    for j in range(k, N // NB):
        parts = [gram_all[p, k, j // 2, 2 * (j % 2) + h] for h in range(2) for p in range(2)]
        block = jnp.concatenate(parts, axis=0)
        cols = slice(NB * j, NB * j + NB)
        x[rows, cols] = block if k == 0 else x[rows, cols] + block


def chol_step(x, k):
    r = lax.broadcasted_iota(jnp.int32, (NB, NB), 0)
    c = lax.broadcasted_iota(jnp.int32, (NB, NB), 1)
    a, b = NB * k, NB * k + NB
    block = factor_block(x[a:b, a:b] + jnp.where(r == c, RIDGE, 0.0))
    low = jnp.where(r >= c, block, 0.0)
    x[a:b, a:b] = low
    low = split(low)
    done, ahead = low, None
    if a:
        left = dot3(low, split(x[a:b, :a]), ((1,), (0,)))
        x[a:b, :a] = left
        done = [jnp.concatenate(pair, axis=1) for pair in zip(split(left), low)]
    if b < N:
        right = dot3(low, split(x[a:b, b:]), ((1,), (0,)))
        x[a:b, b:] = right
        ahead = split(right)
    for i in range(b, N, NB):
        factor = [half[:, i - b : i - b + NB] for half in ahead]
        left = dot3(factor, done, ((0,), (0,)))
        right = dot3(factor, [half[:, i - b :] for half in ahead], ((0,), (0,)))
        x[i : i + NB, a:b] = -left[:, a:]
        if a:
            x[i : i + NB, :a] = x[i : i + NB, :a] - left[:, :a]
            x[i : i + NB, i:] = x[i : i + NB, i:] - right
        else:
            x[i : i + NB, i:] = -right


def main_kernel(
    slab, momentum, basis,
    buffer, right_panel, norm, inner, scaled,
    left_unit, part, total, landed, basis_high, basis_low, panel, from_a, from_b, from_left, from_right,
    from_a2, from_b2, from_left2, from_right2, full, left_panel,
    gram_part, gram_pieces, gram_in, gram_slots, gram_all, x,
    cross_part, cross_in, slots, half_all, mate_half, own_squares, square_slots,
    part_send, part_recv, land_send, land_recv, ring_send, ring_recv, z_send, z_recv,
    pair_send, pair_recv, y_send, y_recv, x_send, x_recv, pass_send, pass_recv, col_send, col_recv,
):
    r, c, p = lax.axis_index("row"), lax.axis_index("col"), lax.axis_index("rep")
    x_at, y_at = c // 4, c % 4
    mate = (r, c, 1 - p)
    sides = {
        "x": ((r, ((x_at + 3) % 4) * 4 + y_at, p), (r, ((x_at + 1) % 4) * 4 + y_at, p)),
        "y": ((r, x_at * 4 + (y_at + 3) % 4, p), (r, x_at * 4 + (y_at + 1) % 4, p)),
    }
    where = {"x": x_at, "y": y_at}
    alone = (c // 8 == p) & (c % 2 == p)

    def peer(step):
        return (r, (c + step) % 16, p)

    def level(step):
        return ((r + step) % 8, c, p)

    barrier = pltpu.get_barrier_semaphore()
    pl.semaphore_signal(barrier, inc=1, device_id=mate, device_id_type=MESH)
    for step in range(1, 16):
        pl.semaphore_signal(barrier, inc=1, device_id=peer(step), device_id_type=MESH)
    for step in range(1, 8):
        pl.semaphore_signal(barrier, inc=1, device_id=level(step), device_id_type=MESH)
    for slot in range(8):
        @pl.when(jnp.logical_not(alone & (8 * p + slot == c)))
        def _():
            pl.semaphore_signal(barrier, inc=1, device_id=(r, 8 * p + slot, c % 2), device_id_type=MESH)
    pl.semaphore_wait(barrier, jnp.where(alone, 30, 31))

    started = []

    first = c // 2
    copies = {}
    for q in range(2):
        for step in range(8):
            b = (first + step) % 8
            cols = pl.ds(pl.multiple_of(512 * (2 * b + 1 - p), 512), 512)
            copy = remote(
                slab.at[0, pl.ds(32 * q, 32), cols], part.at[q, step], part_send.at[q, step], part_recv.at[q, step], mate
            )
            copy.start()
            copies[q, step] = copy
            started.append(copy)

    def block_copy(q, step):
        d = 2 * ((first + step) % 8) + p
        own = (d == c) & (c // 8 == p)
        slot = c % 8
        return own, remote(
            total.at[q, step], landed.at[q, slot], land_send.at[q, step], land_recv.at[q, slot], (r, d, c // 8)
        )

    for q in range(2):
        for step in range(8):
            copies[q, step].wait_recv()
            cols = pl.ds(pl.multiple_of(512 * (2 * ((first + step) % 8) + p), 512), 512)
            total[q, step] = part[q, step] + slab[0, 32 * q : 32 * q + 32, cols]
            own, copy = block_copy(q, step)

            @pl.when(own)
            def _():
                landed[q, c % 8] = total[q, step]

            @pl.when(jnp.logical_not(own))
            def _():
                copy.start()

    high, low = split(basis[...])
    basis_high[...] = high
    basis_low[...] = low

    def land(q):
        for slot in range(8):
            @pl.when(jnp.logical_not(alone & (8 * p + slot == c)))
            def _():
                remote(
                    total.at[q, 0], landed.at[q, slot], land_send.at[q, 0], land_recv.at[q, slot],
                    (r, 8 * p + slot, c % 2),
                ).wait_recv()
            rows = slice(64 * slot + 32 * q, 64 * slot + 32 * q + 32)
            buffer[rows, :] = momentum[rows, :] + landed[q, slot]
        tile = jnp.concatenate([buffer[64 * s + 32 * q : 64 * s + 32 * q + 32, :] for s in range(8)], axis=0)
        tile = split(tile)
        for h in range(2):
            cols = slice(512 * h, 512 * h + 512)
            got = dot3(tile, (basis_high[:, cols], basis_low[:, cols]), ((1,), (0,)))
            for u in range(4):
                for v in range(4):
                    n = 4 * u + v
                    f, s = (u, v) if h == 0 else (v, u)
                    panel[q, h, f, s] = got[16 * n : 16 * n + 16]

    def total_over_col(q, h):
        axis, other = ("x", "y") if h == 0 else ("y", "x")
        f, s = where[axis], where[other]
        yield from ring_scatter(
            lambda i: panel.at[q, h, i],
            lambda i, k: panel.at[q, h, i, pl.ds(2 * k, 2)],
            from_a.at[q, h], from_b.at[q, h], from_left.at[q, h], from_right.at[q, h],
            f, *sides[axis], ring_send.at[q, h, 0], ring_recv.at[q, h, 0], started,
        )
        yield from ring_scatter(
            lambda i: panel.at[q, h, f, i],
            lambda i, k: panel.at[q, h, f, i, pl.ds(8 * k, 8)],
            from_a2.at[q, h], from_b2.at[q, h], from_left2.at[q, h], from_right2.at[q, h],
            s, *sides[other], ring_send.at[q, h, 1], ring_recv.at[q, h, 1], started,
        )
        full[q, h, f, s] = panel[q, h, f, s]
        yield from ring_gather(
            lambda i: full.at[q, h, f, i],
            lambda i, k: full.at[q, h, f, i, pl.ds(8 * k, 8)],
            s, *sides[other], ring_send.at[q, h, 2], ring_recv.at[q, h, 2], started,
        )
        yield from ring_gather(
            lambda i: full.at[q, h, i],
            lambda i, k: full.at[q, h, i, pl.ds(2 * k, 2)],
            f, *sides[axis], ring_send.at[q, h, 3], ring_recv.at[q, h, 3], started,
        )

    sums = {(q, h): total_over_col(q, h) for q in range(2) for h in range(2)}
    for q in range(2):
        land(q)
        for h in range(2):
            next(sums[q, h])
    lockstep(sums[0, 0], sums[0, 1], sums[1, 0], sums[1, 1])
    for q in range(2):
        for u in range(4):
            for v in range(4):
                n = 4 * u + v
                top = 64 * (n // 2) + 32 * q + 16 * (n % 2)
                left_panel[top : top + 16, 0:512] = full[q, 0, u, v]
                left_panel[top : top + 16, 512:1024] = full[q, 1, v, u]

    column = pl.ds(pl.multiple_of(NB * (c // 2), NB), NB)
    left_split = split(left_panel[...])
    gram_part[...] = dot3(left_split, split(left_panel[:, column]), ((0,), (0,)))
    for q in range(2):
        for b in range(8):
            rows = pl.ds(pl.multiple_of(NB * b + 64 * (c % 2) + 32 * q, 32), 32)
            gram_pieces[q, b] = gram_part[rows, :]
    swap = remote(gram_pieces.at[1 - p], gram_in, pair_send.at[0], pair_recv.at[0], mate)
    swap.start()
    started.append(swap)

    def cross(q):
        cross_part[q] = dot3(split(buffer[:, 256 * q : 256 * q + 256]), left_split, ((0,), (0,)))

    swap.wait_recv()
    gram_pieces[p] = gram_pieces[p] + gram_in[...]
    moves = []
    for step in range(1, 8):
        z = (r + step) % 8
        move = remote(gram_pieces.at[p, z], gram_slots.at[r], z_send.at[0, step], z_recv.at[0, step], level(step))
        move.start()
        moves.append(move)
    started += moves
    gram_slots[r] = gram_pieces[p, r]
    cross(0)
    for move in moves:
        move.wait_recv()
    acc = gram_slots[0]
    for z in range(1, 8):
        acc = acc + gram_slots[z]
    gram_all[p, r, x_at, y_at] = acc
    moves = []
    for step in range(1, 8):
        own = gram_all.at[p, r, x_at, y_at]
        move = remote(own, own, z_send.at[1, step], z_recv.at[1, step], level(step))
        move.start()
        moves.append(move)
    started += moves
    cross(1)
    cross_swap = remote(cross_part.at[1 - p], cross_in, pair_send.at[1], pair_recv.at[1], mate)
    cross_swap.start()
    started.append(cross_swap)
    for move in moves:
        move.wait_recv()

    direct = (0, 1)

    def along_y(part, step):
        own = gram_all.at[p, pl.ds(part, 1 + 6 * part), x_at, y_at]
        device = (r, 4 * x_at + (y_at + step) % 4, p)
        return remote(own, own, y_send.at[part, step], y_recv.at[part, step], device)

    def along_x(b, step, other=0):
        own = gram_all.at[p, b, x_at]
        device = (r, 4 * ((x_at + step) % 4) + y_at, (p + other) % 2)
        index = 8 * other + b
        return remote(own, own, x_send.at[index, step], x_recv.at[index, step], device)

    def x_start(b):
        @pl.when(2 * x_at + 1 >= b)
        def _():
            for step in range(1, 4):
                along_x(b, step).start()
            if b in direct:
                for step in range(4):
                    along_x(b, step, 1).start()

    def x_wait(b):
        for step in range(1, 4):
            @pl.when(2 * ((x_at + 4 - step) % 4) + 1 >= b)
            def _():
                along_x(b, step).wait_recv()
        if b in direct:
            for step in range(4):
                along_x(b, step, 1).wait_recv()

    passed = {}

    def x_pass(b):
        view = gram_all.at[p, b, pl.ds(b // 2, 4 - b // 2)]
        passed[b] = remote(view, view, pass_send.at[b], pass_recv.at[b], mate)
        passed[b].start()
        started.append(passed[b])

    def rows_of(z):
        return pl.ds(pl.multiple_of(32 * z, 32), 32)

    for part in range(2):
        for step in range(1, 4):
            along_y(part, step).start()
    for step in range(1, 4):
        along_y(0, step).wait_recv()
    x_start(0)
    for step in range(1, 4):
        along_y(1, step).wait_recv()
    x_start(1)
    x_start(2)
    moves = []
    handed = {}

    def hand(step):
        view = half_all.at[rows_of((r + 8 - step) % 8)]
        into = mate_half.at[rows_of((r + 8 - step) % 8)]
        handed[step] = remote(view, into, pass_send.at[8 + step], pass_recv.at[8 + step], mate)
        handed[step].start()
        started.append(handed[step])

    for k in range(8):
        if k in direct:
            x_wait(k)
        else:
            passed[k].wait_recv()
        if k + 1 < 8 and k + 1 not in direct:
            x_wait(k + 1)
            x_pass(k + 1)
        if k + 3 < 8:
            x_start(k + 3)
        if k == 0:
            cross_swap.wait_recv()
            cross_part[p] = cross_part[p] + cross_in[...]
            for step in range(1, 8):
                z = (r + step) % 8
                move = remote(cross_part.at[p, rows_of(z)], slots.at[r], z_send.at[2, step], z_recv.at[2, step], level(step))
                move.start()
                moves.append(move)
            started += moves
            slots[r] = cross_part[p, rows_of(r), :]
        if k == 4:
            for move in moves:
                move.wait_recv()
            acc = slots[0]
            for z in range(1, 8):
                acc = acc + slots[z]
            own_rows = half_all.at[rows_of(r)]
            own_rows[...] = acc
            moves = []
            for step in range(1, 8):
                move = remote(own_rows, own_rows, z_send.at[3, step], z_recv.at[3, step], level(step))
                move.start()
                moves.append(move)
            started += moves
            hand(0)
        if k == 7:
            for step in (1, 7, 2, 6):
                moves[step - 1].wait_recv()
                hand(step)
        place_rows(x, gram_all, k)
        chol_step(x, k)

    for step in (3, 5, 4):
        moves[step - 1].wait_recv()
        hand(step)

    rows = lax.broadcasted_iota(jnp.int32, (256, 256), 0)
    cols = lax.broadcasted_iota(jnp.int32, (256, 256), 1)
    bands = []
    for j in range(4):
        band = x[256 * j : 256 * j + 256, : 256 * j + 256]
        corner = jnp.where(rows >= cols, band[:, 256 * j :], 0.0)
        bands.append(split(jnp.concatenate([band[:, : 256 * j], corner], axis=1) if j else corner))

    def solve(panel_split, out, at):
        for j in range(4):
            n = 256 * j + 256
            out[at, 256 * j : n] = dot3((panel_split[0][:, :n], panel_split[1][:, :n]), bands[j], ((1,), (1,)))

    for step in range(8):
        handed[step].wait_recv()
    for q in range(2):
        @pl.when(p == q)
        def _():
            solve(split(half_all[...]), right_panel, slice(256 * q, 256 * q + 256))
            solve(split(mate_half[...]), right_panel, slice(256 - 256 * q, 512 - 256 * q))
    v = right_panel[...]
    square_sums = jnp.sum(v * v, axis=0, keepdims=True)
    for k in range(8):
        own_squares[k : k + 1, :] = square_sums[:, 128 * k : 128 * k + 128]
    square_slots[c] = own_squares[...]
    moves = []
    for step in range(1, 16):
        move = remote(own_squares, square_slots.at[c], col_send.at[step], col_recv.at[step], peer(step))
        move.start()
        moves.append(move)
    started += moves
    solve(split(left_panel[...]), left_unit, slice(0, 512))
    unit = split(left_unit[...])
    inner[...] = dot3(unit, split(right_panel[...]), ((1,), (1,)))
    for move in moves:
        move.wait_recv()
    acc = square_slots[0]
    for i in range(1, 16):
        acc = acc + square_slots[i]
    norms = jnp.sqrt(acc + EPSILON)
    for k in range(8):
        norm[:, 128 * k : 128 * k + 128] = norms[k : k + 1, :]
    scaled[...] = dot3(unit, split(right_panel[...] / norm[...]), ((1,), (1,)))

    for move in started:
        move.wait_send()
    for q in range(2):
        for step in range(8):
            own, copy = block_copy(q, step)

            @pl.when(jnp.logical_not(own))
            def _():
                copy.wait_send()
    for part in range(2):
        for step in range(1, 4):
            along_y(part, step).wait_send()
    for b in range(8):
        @pl.when(2 * x_at + 1 >= b)
        def _():
            for step in range(1, 4):
                along_x(b, step).wait_send()
            if b in direct:
                for step in range(4):
                    along_x(b, step, 1).wait_send()


def panels(gradients, momentum, right_basis):
    f32 = jnp.float32
    vmem = pl.BlockSpec(memory_space=pltpu.VMEM)
    dma = pltpu.SemaphoreType.DMA
    return pl.pallas_call(
        main_kernel,
        out_shape=[
            jax.ShapeDtypeStruct((512, 512), f32),
            jax.ShapeDtypeStruct((512, N), f32),
            jax.ShapeDtypeStruct((1, N), f32),
            jax.ShapeDtypeStruct((512, 512), f32),
            jax.ShapeDtypeStruct((512, 512), f32),
        ],
        in_specs=[vmem] * 3,
        out_specs=[vmem] * 5,
        scratch_shapes=[
            pltpu.VMEM((512, N), f32),
            pltpu.VMEM((2, 8, 32, 512), f32),
            pltpu.VMEM((2, 8, 32, 512), f32),
            pltpu.VMEM((2, 8, 32, 512), f32),
            pltpu.VMEM((512, N), jnp.bfloat16),
            pltpu.VMEM((512, N), jnp.bfloat16),
            pltpu.VMEM((2, 2, 4, 4, 16, 512), f32),
            pltpu.VMEM((2, 2, 2, 16, 512), f32),
            pltpu.VMEM((2, 2, 2, 16, 512), f32),
            pltpu.VMEM((2, 2, 4, 16, 512), f32),
            pltpu.VMEM((2, 2, 4, 16, 512), f32),
            pltpu.VMEM((2, 2, 8, 512), f32),
            pltpu.VMEM((2, 2, 8, 512), f32),
            pltpu.VMEM((2, 2, 16, 512), f32),
            pltpu.VMEM((2, 2, 16, 512), f32),
            pltpu.VMEM((2, 2, 4, 4, 16, 512), f32),
            pltpu.VMEM((512, N), f32),
            pltpu.VMEM((N, NB), f32),
            pltpu.VMEM((2, 8, 32, NB), f32),
            pltpu.VMEM((8, 32, NB), f32),
            pltpu.VMEM((8, 32, NB), f32),
            pltpu.VMEM((2, 8, 4, 4, 32, NB), f32),
            pltpu.VMEM((N, N), f32),
            pltpu.VMEM((2, 256, N), f32),
            pltpu.VMEM((256, N), f32),
            pltpu.VMEM((8, 32, N), f32),
            pltpu.VMEM((256, N), f32),
            pltpu.VMEM((256, N), f32),
            pltpu.VMEM((8, 128), f32),
            pltpu.VMEM((16, 8, 128), f32),
            dma((2, 8)), dma((2, 8)), dma((2, 8)), dma((2, 8)),
            dma((2, 2, 4, 4)), dma((2, 2, 4, 4)),
            dma((4, 8)), dma((4, 8)),
            dma((2,)), dma((2,)),
            dma((2, 4)), dma((2, 4)),
            dma((16, 4)), dma((16, 4)),
            dma((16,)), dma((16,)),
            dma((16,)), dma((16,)),
        ],
        compiler_params=pltpu.CompilerParams(collective_id=0, has_side_effects=True, vmem_limit_bytes=56 << 20),
    )(gradients, momentum, right_basis)


def shards(gradients, momentum, right_basis):
    buffer, right_panel, norm, inner, scaled = panels(gradients, momentum, right_basis)
    new_basis = right_panel / norm
    new_momentum = buffer - (1.0 - DECAY) * inner
    update = (D / math.sqrt(N)) * scaled
    return (new_momentum, new_basis, update)


def solution(mesh):
    return jax.shard_map(
        shards,
        mesh=mesh,
        in_specs=(P("rep", ("row", "col"), None), P(("row", "rep"), "col"), P("col", None)),
        out_specs=(P(("row", "rep"), "col"), P("col", None), P(("row", "rep"), "col")),
        check_vma=False,
    )
```

```python
import functools
import math

import jax
import jax.numpy as jnp
from jax import lax
from jax.experimental import pallas as pl
from jax.experimental.pallas import tpu as pltpu
from jax.sharding import PartitionSpec as P

N = 1024
NB = 128
HI = lax.Precision.HIGHEST
EPSILON = 1e-06
RIDGE = 0.001
DECAY = 0.95
D = 8192
MESH = pl.DeviceIdType.MESH


def dot(left, right, dims, precision=HI):
    return lax.dot_general(left, right, (dims, ((), ())), precision=precision, preferred_element_type=jnp.float32)


def split(a):
    high = a.astype(jnp.bfloat16)
    return high, (a - high.astype(jnp.float32)).astype(jnp.bfloat16)


def dot3(left, right, dims):
    def one(a, b):
        return lax.dot_general(a, b, (dims, ((), ())), preferred_element_type=jnp.float32)

    return one(left[0], right[0]) + (one(left[0], right[1]) + one(left[1], right[0]))


def factor_block(rest):
    lane = lax.broadcasted_iota(jnp.int32, (8, NB), 1)
    sub = lax.broadcasted_iota(jnp.int32, (8, NB), 0)
    done = []
    for base in range(0, NB, 8):
        top, rest = rest[:8], rest[8:]
        n = rest.shape[0]
        inside = (lane >= base) & (lane < base + 8)
        pivots = [jnp.broadcast_to(top[:, base + k : base + k + 1], (8, NB)) for k in range(8)]
        top = jnp.where(inside, jnp.where(lane - base == sub, 1.0, 0.0), top)
        if n:
            below = [jnp.broadcast_to(rest[:, base + k : base + k + 1], (n, NB)) for k in range(8)]
            wide = lax.broadcasted_iota(jnp.int32, (n, NB), 1)
            rest = jnp.where((wide >= base) & (wide < base + 8), 0.0, rest)
        for k in range(8):
            scale = lax.rsqrt(pivots[k][k : k + 1, :])
            row = top[k : k + 1, :] * scale
            factor = jnp.where(sub > k, pivots[k] * scale, 0.0)
            top = jnp.where(sub == k, row, top - factor * row)
            cross = {}
            for q in range(k + 1, 8):
                cross[q] = pivots[q][k : k + 1, :] * scale
                pivots[q] = pivots[q] - factor * cross[q]
            if n:
                lower = below[k] * scale
                rest = rest - lower * row
                for q in range(k + 1, 8):
                    below[q] = below[q] - lower * cross[q]
        done.append(top)
    return jnp.concatenate(done, axis=0)


def remote(src, dst, send, recv, device):
    return pltpu.make_async_remote_copy(
        src_ref=src, dst_ref=dst, send_sem=send, recv_sem=recv, device_id=device, device_id_type=MESH
    )


def ring_scatter(piece, half, from_a, from_b, from_left, from_right, pos, left, right, send, recv, started):
    before, after, across = (pos + 3) % 4, (pos + 1) % 4, (pos + 2) % 4
    a = remote(half(across, 0), from_a, send.at[0], recv.at[0], left)
    b = remote(half(across, 1), from_b, send.at[1], recv.at[1], right)
    a.start()
    b.start()
    yield
    a.wait_recv()
    half(before, 0)[...] = half(before, 0)[...] + from_a[...]
    c = remote(piece(before), from_right, send.at[2], recv.at[2], left)
    c.start()
    b.wait_recv()
    half(after, 1)[...] = half(after, 1)[...] + from_b[...]
    d = remote(piece(after), from_left, send.at[3], recv.at[3], right)
    d.start()
    yield
    c.wait_recv()
    d.wait_recv()
    piece(pos)[...] = piece(pos)[...] + (from_left[...] + from_right[...])
    started += [a, b, c, d]


def ring_gather(piece, half, pos, left, right, send, recv, started, done=None):
    before, after, across = (pos + 3) % 4, (pos + 1) % 4, (pos + 2) % 4
    a = remote(piece(pos), piece(pos), send.at[0], recv.at[0], left)
    b = remote(piece(pos), piece(pos), send.at[1], recv.at[1], right)
    a.start()
    b.start()
    if done:
        done(0, pos)
    yield
    a.wait_recv()
    c = remote(half(after, 0), half(after, 0), send.at[2], recv.at[2], left)
    c.start()
    b.wait_recv()
    d = remote(half(before, 1), half(before, 1), send.at[3], recv.at[3], right)
    d.start()
    if done:
        done(1, after)
        done(2, before)
    yield
    c.wait_recv()
    d.wait_recv()
    if done:
        done(3, across)
    started += [a, b, c, d]


def lockstep(*stages):
    stages = list(stages)
    while stages:
        for stage in list(stages):
            try:
                next(stage)
            except StopIteration:
                stages.remove(stage)


def place_rows(x, gram_all, k):
    rows = slice(NB * k, NB * k + NB)
    for j in range(k, N // NB):
        parts = [gram_all[p, k, j // 2, 2 * (j % 2) + h] for h in range(2) for p in range(2)]
        block = jnp.concatenate(parts, axis=0)
        cols = slice(NB * j, NB * j + NB)
        x[rows, cols] = block if k == 0 else x[rows, cols] + block


def chol_step(x, k):
    r = lax.broadcasted_iota(jnp.int32, (NB, NB), 0)
    c = lax.broadcasted_iota(jnp.int32, (NB, NB), 1)
    a, b = NB * k, NB * k + NB
    block = factor_block(x[a:b, a:b] + jnp.where(r == c, RIDGE, 0.0))
    low = jnp.where(r >= c, block, 0.0)
    x[a:b, a:b] = low
    low = split(low)
    done, ahead = low, None
    if a:
        left = dot3(low, split(x[a:b, :a]), ((1,), (0,)))
        x[a:b, :a] = left
        done = [jnp.concatenate(pair, axis=1) for pair in zip(split(left), low)]
    if b < N:
        right = dot3(low, split(x[a:b, b:]), ((1,), (0,)))
        x[a:b, b:] = right
        ahead = split(right)
    for i in range(b, N, NB):
        factor = [half[:, i - b : i - b + NB] for half in ahead]
        left = dot3(factor, done, ((0,), (0,)))
        right = dot3(factor, [half[:, i - b :] for half in ahead], ((0,), (0,)))
        x[i : i + NB, a:b] = -left[:, a:]
        if a:
            x[i : i + NB, :a] = x[i : i + NB, :a] - left[:, :a]
            x[i : i + NB, i:] = x[i : i + NB, i:] - right
        else:
            x[i : i + NB, i:] = -right


def main_kernel(
    slab, momentum, basis,
    buffer, right_panel, norm, inner, scaled,
    left_unit, part, total, landed, basis_high, basis_low, panel, from_a, from_b, from_left, from_right,
    from_a2, from_b2, from_left2, from_right2, full, left_panel,
    gram_part, gram_pieces, gram_in, gram_slots, gram_all, x,
    cross_part, cross_in, down_sums, up_sums, half_all, mate_half, own_squares, square_slots,
    part_send, part_recv, land_send, land_recv, ring_send, ring_recv, z_send, z_recv,
    pair_send, pair_recv, y_send, y_recv, x_send, x_recv, pass_send, pass_recv, col_send, col_recv,
):
    r, c, p = lax.axis_index("row"), lax.axis_index("col"), lax.axis_index("rep")
    x_at, y_at = c // 4, c % 4
    mate = (r, c, 1 - p)
    sides = {
        "x": ((r, ((x_at + 3) % 4) * 4 + y_at, p), (r, ((x_at + 1) % 4) * 4 + y_at, p)),
        "y": ((r, x_at * 4 + (y_at + 3) % 4, p), (r, x_at * 4 + (y_at + 1) % 4, p)),
    }
    where = {"x": x_at, "y": y_at}
    alone = (c // 8 == p) & (c % 2 == p)

    def peer(step):
        return (r, (c + step) % 16, p)

    def level(step):
        return ((r + step) % 8, c, p)

    barrier = pltpu.get_barrier_semaphore()
    pl.semaphore_signal(barrier, inc=1, device_id=mate, device_id_type=MESH)
    for step in range(1, 16):
        pl.semaphore_signal(barrier, inc=1, device_id=peer(step), device_id_type=MESH)
    for step in range(1, 8):
        pl.semaphore_signal(barrier, inc=1, device_id=level(step), device_id_type=MESH)
    for slot in range(8):
        @pl.when(jnp.logical_not(alone & (8 * p + slot == c)))
        def _():
            pl.semaphore_signal(barrier, inc=1, device_id=(r, 8 * p + slot, c % 2), device_id_type=MESH)
    pl.semaphore_wait(barrier, jnp.where(alone, 30, 31))

    started = []

    first = c // 2
    copies = {}
    for q in range(2):
        for step in range(8):
            b = (first + step) % 8
            cols = pl.ds(pl.multiple_of(512 * (2 * b + 1 - p), 512), 512)
            copy = remote(
                slab.at[0, pl.ds(32 * q, 32), cols], part.at[q, step], part_send.at[q, step], part_recv.at[q, step], mate
            )
            copy.start()
            copies[q, step] = copy
            started.append(copy)

    def block_copy(q, step):
        d = 2 * ((first + step) % 8) + p
        own = (d == c) & (c // 8 == p)
        slot = c % 8
        return own, remote(
            total.at[q, step], landed.at[q, slot], land_send.at[q, step], land_recv.at[q, slot], (r, d, c // 8)
        )

    for q in range(2):
        for step in range(8):
            copies[q, step].wait_recv()
            cols = pl.ds(pl.multiple_of(512 * (2 * ((first + step) % 8) + p), 512), 512)
            total[q, step] = part[q, step] + slab[0, 32 * q : 32 * q + 32, cols]
            own, copy = block_copy(q, step)

            @pl.when(own)
            def _():
                landed[q, c % 8] = total[q, step]

            @pl.when(jnp.logical_not(own))
            def _():
                copy.start()

    high, low = split(basis[...])
    basis_high[...] = high
    basis_low[...] = low

    def land(q):
        for slot in range(8):
            @pl.when(jnp.logical_not(alone & (8 * p + slot == c)))
            def _():
                remote(
                    total.at[q, 0], landed.at[q, slot], land_send.at[q, 0], land_recv.at[q, slot],
                    (r, 8 * p + slot, c % 2),
                ).wait_recv()
            rows = slice(64 * slot + 32 * q, 64 * slot + 32 * q + 32)
            buffer[rows, :] = momentum[rows, :] + landed[q, slot]
        tile = jnp.concatenate([buffer[64 * s + 32 * q : 64 * s + 32 * q + 32, :] for s in range(8)], axis=0)
        tile = split(tile)
        for h in range(2):
            cols = slice(512 * h, 512 * h + 512)
            got = dot3(tile, (basis_high[:, cols], basis_low[:, cols]), ((1,), (0,)))
            for u in range(4):
                for v in range(4):
                    n = 4 * u + v
                    f, s = (u, v) if h == 0 else (v, u)
                    panel[q, h, f, s] = got[16 * n : 16 * n + 16]

    def total_over_col(q, h):
        axis, other = ("x", "y") if h == 0 else ("y", "x")
        f, s = where[axis], where[other]
        yield from ring_scatter(
            lambda i: panel.at[q, h, i],
            lambda i, k: panel.at[q, h, i, pl.ds(2 * k, 2)],
            from_a.at[q, h], from_b.at[q, h], from_left.at[q, h], from_right.at[q, h],
            f, *sides[axis], ring_send.at[q, h, 0], ring_recv.at[q, h, 0], started,
        )
        yield from ring_scatter(
            lambda i: panel.at[q, h, f, i],
            lambda i, k: panel.at[q, h, f, i, pl.ds(8 * k, 8)],
            from_a2.at[q, h], from_b2.at[q, h], from_left2.at[q, h], from_right2.at[q, h],
            s, *sides[other], ring_send.at[q, h, 1], ring_recv.at[q, h, 1], started,
        )
        full[q, h, f, s] = panel[q, h, f, s]
        yield from ring_gather(
            lambda i: full.at[q, h, f, i],
            lambda i, k: full.at[q, h, f, i, pl.ds(8 * k, 8)],
            s, *sides[other], ring_send.at[q, h, 2], ring_recv.at[q, h, 2], started,
        )
        yield from ring_gather(
            lambda i: full.at[q, h, i],
            lambda i, k: full.at[q, h, i, pl.ds(2 * k, 2)],
            f, *sides[axis], ring_send.at[q, h, 3], ring_recv.at[q, h, 3], started,
        )

    sums = {(q, h): total_over_col(q, h) for q in range(2) for h in range(2)}
    for q in range(2):
        land(q)
        for h in range(2):
            next(sums[q, h])
    lockstep(sums[0, 0], sums[0, 1], sums[1, 0], sums[1, 1])
    for q in range(2):
        for u in range(4):
            for v in range(4):
                n = 4 * u + v
                top = 64 * (n // 2) + 32 * q + 16 * (n % 2)
                left_panel[top : top + 16, 0:512] = full[q, 0, u, v]
                left_panel[top : top + 16, 512:1024] = full[q, 1, v, u]

    column = pl.ds(pl.multiple_of(NB * (c // 2), NB), NB)
    left_split = split(left_panel[...])
    gram_part[...] = dot3(left_split, split(left_panel[:, column]), ((0,), (0,)))
    for q in range(2):
        for b in range(8):
            rows = pl.ds(pl.multiple_of(NB * b + 64 * (c % 2) + 32 * q, 32), 32)
            gram_pieces[q, b] = gram_part[rows, :]
    swap = remote(gram_pieces.at[1 - p], gram_in, pair_send.at[0], pair_recv.at[0], mate)
    swap.start()
    started.append(swap)

    def cross(q):
        cross_part[q] = dot3(split(buffer[:, 256 * q : 256 * q + 256]), left_split, ((0,), (0,)))

    swap.wait_recv()
    gram_pieces[p] = gram_pieces[p] + gram_in[...]
    moves = []
    for step in range(1, 8):
        z = (r + step) % 8
        move = remote(gram_pieces.at[p, z], gram_slots.at[r], z_send.at[0, step], z_recv.at[0, step], level(step))
        move.start()
        moves.append(move)
    started += moves
    gram_slots[r] = gram_pieces[p, r]
    cross(0)
    for move in moves:
        move.wait_recv()
    acc = gram_slots[0]
    for z in range(1, 8):
        acc = acc + gram_slots[z]
    gram_all[p, r, x_at, y_at] = acc
    moves = []
    for step in range(1, 8):
        own = gram_all.at[p, r, x_at, y_at]
        move = remote(own, own, z_send.at[1, step], z_recv.at[1, step], level(step))
        move.start()
        moves.append(move)
    started += moves
    cross(1)
    cross_swap = remote(cross_part.at[1 - p], cross_in, pair_send.at[1], pair_recv.at[1], mate)
    cross_swap.start()
    started.append(cross_swap)
    for move in moves:
        move.wait_recv()

    direct = (0, 1)

    def along_y(part, step):
        own = gram_all.at[p, pl.ds(part, 1 + 6 * part), x_at, y_at]
        device = (r, 4 * x_at + (y_at + step) % 4, p)
        return remote(own, own, y_send.at[part, step], y_recv.at[part, step], device)

    def along_x(b, step, other=0):
        own = gram_all.at[p, b, x_at]
        device = (r, 4 * ((x_at + step) % 4) + y_at, (p + other) % 2)
        index = 8 * other + b
        return remote(own, own, x_send.at[index, step], x_recv.at[index, step], device)

    def x_start(b):
        @pl.when(2 * x_at + 1 >= b)
        def _():
            for step in range(1, 4):
                along_x(b, step).start()
            if b in direct:
                for step in range(4):
                    along_x(b, step, 1).start()

    def x_wait(b):
        for step in range(1, 4):
            @pl.when(2 * ((x_at + 4 - step) % 4) + 1 >= b)
            def _():
                along_x(b, step).wait_recv()
        if b in direct:
            for step in range(4):
                along_x(b, step, 1).wait_recv()

    passed = {}

    def x_pass(b):
        view = gram_all.at[p, b, pl.ds(b // 2, 4 - b // 2)]
        passed[b] = remote(view, view, pass_send.at[b], pass_recv.at[b], mate)
        passed[b].start()
        started.append(passed[b])

    def rows_of(z):
        return pl.ds(pl.multiple_of(32 * z, 32), 32)

    for part in range(2):
        for step in range(1, 4):
            along_y(part, step).start()
    for step in range(1, 4):
        along_y(0, step).wait_recv()
    x_start(0)
    for step in range(1, 4):
        along_y(1, step).wait_recv()
    x_start(1)
    x_start(2)
    lower, upper = level(7), level(1)
    handed = []

    def hand(z):
        rows = rows_of(z)
        copy = remote(half_all.at[rows], mate_half.at[rows], pass_send.at[8 + len(handed)], pass_recv.at[8 + len(handed)], mate)
        copy.start()
        handed.append(copy)
        started.append(copy)

    def row_piece(offset):
        return cross_part.at[p, rows_of((r + 8 + offset) % 8)]

    def hop(src, dst, index, device):
        copy = remote(src, dst, z_send.at[2 + index // 8, index % 8], z_recv.at[2 + index // 8, index % 8], device)
        copy.start()
        started.append(copy)
        return copy

    def cross_sum():
        cross_swap.wait_recv()
        cross_part[p] = cross_part[p] + cross_in[...]
        a = hop(row_piece(-4), down_sums.at[0], 0, lower)
        yield
        a.wait_recv()
        down_sums[0] = down_sums[0] + row_piece(-3)[...]
        a = hop(down_sums.at[0], down_sums.at[1], 1, lower)
        b = hop(row_piece(3), up_sums.at[0], 4, upper)
        yield
        for step in (1, 2):
            a.wait_recv()
            down_sums[step] = down_sums[step] + row_piece(step - 3)[...]
            a = hop(down_sums.at[step], down_sums.at[step + 1], 1 + step, lower)
            b.wait_recv()
            up_sums[step - 1] = up_sums[step - 1] + row_piece(3 - step)[...]
            b = hop(up_sums.at[step - 1], up_sums.at[step], 4 + step, upper)
            yield
        a.wait_recv()
        b.wait_recv()
        own = half_all.at[rows_of(r)]
        own[...] = row_piece(0)[...] + (down_sums[3] + up_sums[2])
        a = hop(own, own, 8, lower)
        b = hop(own, own, 9, upper)
        hand(r)
        yield
        for step in (1, 2, 3):
            a.wait_recv()
            view = half_all.at[rows_of((r + step) % 8)]
            a = hop(view, view, 8 + 2 * step, lower)
            b.wait_recv()
            if step < 3:
                view = half_all.at[rows_of((r + 8 - step) % 8)]
                b = hop(view, view, 9 + 2 * step, upper)
            hand((r + step) % 8)
            hand((r + 8 - step) % 8)
            yield
        a.wait_recv()
        hand((r + 4) % 8)
        yield

    crossing = cross_sum()
    next(crossing)
    for k in range(8):
        if k in direct:
            x_wait(k)
        else:
            passed[k].wait_recv()
        if k + 1 < 8 and k + 1 not in direct:
            x_wait(k + 1)
            x_pass(k + 1)
        if k + 3 < 8:
            x_start(k + 3)
        next(crossing)
        place_rows(x, gram_all, k)
        chol_step(x, k)

    rows = lax.broadcasted_iota(jnp.int32, (256, 256), 0)
    cols = lax.broadcasted_iota(jnp.int32, (256, 256), 1)
    bands = []
    for j in range(4):
        band = x[256 * j : 256 * j + 256, : 256 * j + 256]
        corner = jnp.where(rows >= cols, band[:, 256 * j :], 0.0)
        bands.append(split(jnp.concatenate([band[:, : 256 * j], corner], axis=1) if j else corner))

    def solve(panel_split, out, at):
        for j in range(4):
            n = 256 * j + 256
            out[at, 256 * j : n] = dot3((panel_split[0][:, :n], panel_split[1][:, :n]), bands[j], ((1,), (1,)))

    for copy in handed:
        copy.wait_recv()
    for q in range(2):
        @pl.when(p == q)
        def _():
            solve(split(half_all[...]), right_panel, slice(256 * q, 256 * q + 256))
            solve(split(mate_half[...]), right_panel, slice(256 - 256 * q, 512 - 256 * q))
    v = right_panel[...]
    square_sums = jnp.sum(v * v, axis=0, keepdims=True)
    for k in range(8):
        own_squares[k : k + 1, :] = square_sums[:, 128 * k : 128 * k + 128]
    square_slots[c] = own_squares[...]
    moves = []
    for step in range(1, 16):
        move = remote(own_squares, square_slots.at[c], col_send.at[step], col_recv.at[step], peer(step))
        move.start()
        moves.append(move)
    started += moves
    solve(split(left_panel[...]), left_unit, slice(0, 512))
    unit = split(left_unit[...])
    inner[...] = dot3(unit, split(right_panel[...]), ((1,), (1,)))
    for move in moves:
        move.wait_recv()
    acc = square_slots[0]
    for i in range(1, 16):
        acc = acc + square_slots[i]
    norms = jnp.sqrt(acc + EPSILON)
    for k in range(8):
        norm[:, 128 * k : 128 * k + 128] = norms[k : k + 1, :]
    scaled[...] = dot3(unit, split(right_panel[...] / norm[...]), ((1,), (1,)))

    for move in started:
        move.wait_send()
    for q in range(2):
        for step in range(8):
            own, copy = block_copy(q, step)

            @pl.when(jnp.logical_not(own))
            def _():
                copy.wait_send()
    for part in range(2):
        for step in range(1, 4):
            along_y(part, step).wait_send()
    for b in range(8):
        @pl.when(2 * x_at + 1 >= b)
        def _():
            for step in range(1, 4):
                along_x(b, step).wait_send()
            if b in direct:
                for step in range(4):
                    along_x(b, step, 1).wait_send()


def panels(gradients, momentum, right_basis):
    f32 = jnp.float32
    vmem = pl.BlockSpec(memory_space=pltpu.VMEM)
    dma = pltpu.SemaphoreType.DMA
    return pl.pallas_call(
        main_kernel,
        out_shape=[
            jax.ShapeDtypeStruct((512, 512), f32),
            jax.ShapeDtypeStruct((512, N), f32),
            jax.ShapeDtypeStruct((1, N), f32),
            jax.ShapeDtypeStruct((512, 512), f32),
            jax.ShapeDtypeStruct((512, 512), f32),
        ],
        in_specs=[vmem] * 3,
        out_specs=[vmem] * 5,
        scratch_shapes=[
            pltpu.VMEM((512, N), f32),
            pltpu.VMEM((2, 8, 32, 512), f32),
            pltpu.VMEM((2, 8, 32, 512), f32),
            pltpu.VMEM((2, 8, 32, 512), f32),
            pltpu.VMEM((512, N), jnp.bfloat16),
            pltpu.VMEM((512, N), jnp.bfloat16),
            pltpu.VMEM((2, 2, 4, 4, 16, 512), f32),
            pltpu.VMEM((2, 2, 2, 16, 512), f32),
            pltpu.VMEM((2, 2, 2, 16, 512), f32),
            pltpu.VMEM((2, 2, 4, 16, 512), f32),
            pltpu.VMEM((2, 2, 4, 16, 512), f32),
            pltpu.VMEM((2, 2, 8, 512), f32),
            pltpu.VMEM((2, 2, 8, 512), f32),
            pltpu.VMEM((2, 2, 16, 512), f32),
            pltpu.VMEM((2, 2, 16, 512), f32),
            pltpu.VMEM((2, 2, 4, 4, 16, 512), f32),
            pltpu.VMEM((512, N), f32),
            pltpu.VMEM((N, NB), f32),
            pltpu.VMEM((2, 8, 32, NB), f32),
            pltpu.VMEM((8, 32, NB), f32),
            pltpu.VMEM((8, 32, NB), f32),
            pltpu.VMEM((2, 8, 4, 4, 32, NB), f32),
            pltpu.VMEM((N, N), f32),
            pltpu.VMEM((2, 256, N), f32),
            pltpu.VMEM((256, N), f32),
            pltpu.VMEM((4, 32, N), f32),
            pltpu.VMEM((3, 32, N), f32),
            pltpu.VMEM((256, N), f32),
            pltpu.VMEM((256, N), f32),
            pltpu.VMEM((8, 128), f32),
            pltpu.VMEM((16, 8, 128), f32),
            dma((2, 8)), dma((2, 8)), dma((2, 8)), dma((2, 8)),
            dma((2, 2, 4, 4)), dma((2, 2, 4, 4)),
            dma((4, 8)), dma((4, 8)),
            dma((2,)), dma((2,)),
            dma((2, 4)), dma((2, 4)),
            dma((16, 4)), dma((16, 4)),
            dma((16,)), dma((16,)),
            dma((16,)), dma((16,)),
        ],
        compiler_params=pltpu.CompilerParams(collective_id=0, has_side_effects=True, vmem_limit_bytes=56 << 20),
    )(gradients, momentum, right_basis)


def shards(gradients, momentum, right_basis):
    buffer, right_panel, norm, inner, scaled = panels(gradients, momentum, right_basis)
    new_basis = right_panel / norm
    new_momentum = buffer - (1.0 - DECAY) * inner
    update = (D / math.sqrt(N)) * scaled
    return (new_momentum, new_basis, update)


def solution(mesh):
    return jax.shard_map(
        shards,
        mesh=mesh,
        in_specs=(P("rep", ("row", "col"), None), P(("row", "rep"), "col"), P("col", None)),
        out_specs=(P(("row", "rep"), "col"), P("col", None), P(("row", "rep"), "col")),
        check_vma=False,
    )
```

```python
import functools
import math

import jax
import jax.numpy as jnp
from jax import lax
from jax.experimental import pallas as pl
from jax.experimental.pallas import tpu as pltpu
from jax.sharding import PartitionSpec as P

N = 1024
NB = 128
HI = lax.Precision.HIGHEST
EPSILON = 1e-06
RIDGE = 0.001
DECAY = 0.95
D = 8192
MESH = pl.DeviceIdType.MESH


def dot(left, right, dims, precision=HI):
    return lax.dot_general(left, right, (dims, ((), ())), precision=precision, preferred_element_type=jnp.float32)


def split(a):
    high = a.astype(jnp.bfloat16)
    return high, (a - high.astype(jnp.float32)).astype(jnp.bfloat16)


def dot3(left, right, dims):
    def one(a, b):
        return lax.dot_general(a, b, (dims, ((), ())), preferred_element_type=jnp.float32)

    return one(left[0], right[0]) + (one(left[0], right[1]) + one(left[1], right[0]))


def factor_block(rest):
    lane = lax.broadcasted_iota(jnp.int32, (8, NB), 1)
    sub = lax.broadcasted_iota(jnp.int32, (8, NB), 0)
    done = []
    for base in range(0, NB, 8):
        top, rest = rest[:8], rest[8:]
        n = rest.shape[0]
        inside = (lane >= base) & (lane < base + 8)
        pivots = [jnp.broadcast_to(top[:, base + k : base + k + 1], (8, NB)) for k in range(8)]
        top = jnp.where(inside, jnp.where(lane - base == sub, 1.0, 0.0), top)
        if n:
            below = [jnp.broadcast_to(rest[:, base + k : base + k + 1], (n, NB)) for k in range(8)]
            wide = lax.broadcasted_iota(jnp.int32, (n, NB), 1)
            rest = jnp.where((wide >= base) & (wide < base + 8), 0.0, rest)
        for k in range(8):
            scale = lax.rsqrt(pivots[k][k : k + 1, :])
            row = top[k : k + 1, :] * scale
            factor = jnp.where(sub > k, pivots[k] * scale, 0.0)
            top = jnp.where(sub == k, row, top - factor * row)
            cross = {}
            for q in range(k + 1, 8):
                cross[q] = pivots[q][k : k + 1, :] * scale
                pivots[q] = pivots[q] - factor * cross[q]
            if n:
                lower = below[k] * scale
                rest = rest - lower * row
                for q in range(k + 1, 8):
                    below[q] = below[q] - lower * cross[q]
        done.append(top)
    return jnp.concatenate(done, axis=0)


def remote(src, dst, send, recv, device):
    return pltpu.make_async_remote_copy(
        src_ref=src, dst_ref=dst, send_sem=send, recv_sem=recv, device_id=device, device_id_type=MESH
    )


def ring_scatter(piece, half, from_a, from_b, from_left, from_right, pos, left, right, send, recv, started):
    before, after, across = (pos + 3) % 4, (pos + 1) % 4, (pos + 2) % 4
    a = remote(half(across, 0), from_a, send.at[0], recv.at[0], left)
    b = remote(half(across, 1), from_b, send.at[1], recv.at[1], right)
    a.start()
    b.start()
    yield
    a.wait_recv()
    half(before, 0)[...] = half(before, 0)[...] + from_a[...]
    c = remote(piece(before), from_right, send.at[2], recv.at[2], left)
    c.start()
    b.wait_recv()
    half(after, 1)[...] = half(after, 1)[...] + from_b[...]
    d = remote(piece(after), from_left, send.at[3], recv.at[3], right)
    d.start()
    yield
    c.wait_recv()
    d.wait_recv()
    piece(pos)[...] = piece(pos)[...] + (from_left[...] + from_right[...])
    started += [a, b, c, d]


def ring_gather(piece, half, pos, left, right, send, recv, started, done=None):
    before, after, across = (pos + 3) % 4, (pos + 1) % 4, (pos + 2) % 4
    a = remote(piece(pos), piece(pos), send.at[0], recv.at[0], left)
    b = remote(piece(pos), piece(pos), send.at[1], recv.at[1], right)
    a.start()
    b.start()
    if done:
        done(0, pos)
    yield
    a.wait_recv()
    c = remote(half(after, 0), half(after, 0), send.at[2], recv.at[2], left)
    c.start()
    b.wait_recv()
    d = remote(half(before, 1), half(before, 1), send.at[3], recv.at[3], right)
    d.start()
    if done:
        done(1, after)
        done(2, before)
    yield
    c.wait_recv()
    d.wait_recv()
    if done:
        done(3, across)
    started += [a, b, c, d]


def lockstep(*stages):
    stages = list(stages)
    while stages:
        for stage in list(stages):
            try:
                next(stage)
            except StopIteration:
                stages.remove(stage)


def place_rows(x, gram_all, k):
    rows = slice(NB * k, NB * k + NB)
    for j in range(k, N // NB):
        parts = [gram_all[p, k, j // 2, 2 * (j % 2) + h] for h in range(2) for p in range(2)]
        block = jnp.concatenate(parts, axis=0)
        cols = slice(NB * j, NB * j + NB)
        x[rows, cols] = block if k == 0 else x[rows, cols] + block


def chol_step(x, k):
    r = lax.broadcasted_iota(jnp.int32, (NB, NB), 0)
    c = lax.broadcasted_iota(jnp.int32, (NB, NB), 1)
    a, b = NB * k, NB * k + NB
    block = factor_block(x[a:b, a:b] + jnp.where(r == c, RIDGE, 0.0))
    low = jnp.where(r >= c, block, 0.0)
    x[a:b, a:b] = low
    low = split(low)
    done, ahead = low, None
    if a:
        left = dot3(low, split(x[a:b, :a]), ((1,), (0,)))
        x[a:b, :a] = left
        done = [jnp.concatenate(pair, axis=1) for pair in zip(split(left), low)]
    if b < N:
        right = dot3(low, split(x[a:b, b:]), ((1,), (0,)))
        x[a:b, b:] = right
        ahead = split(right)
    for i in range(b, N, NB):
        factor = [half[:, i - b : i - b + NB] for half in ahead]
        left = dot3(factor, done, ((0,), (0,)))
        right = dot3(factor, [half[:, i - b :] for half in ahead], ((0,), (0,)))
        x[i : i + NB, a:b] = -left[:, a:]
        if a:
            x[i : i + NB, :a] = x[i : i + NB, :a] - left[:, :a]
            x[i : i + NB, i:] = x[i : i + NB, i:] - right
        else:
            x[i : i + NB, i:] = -right


def main_kernel(
    slab, momentum_in, basis_in,
    buffer_out, panel_out, norm, inner_out, scaled,
    momentum, basis, own_blocks, buffer, right_panel, inner, in_sem, block_sem, out_sem,
    left_unit, part, total, landed, basis_high, basis_low, panel, from_a, from_b, from_left, from_right,
    others, full, left_panel, left_high, left_low,
    gram_part, gram_pieces, gram_in, gram_slots, gram_all, x,
    cross_part, cross_in, down_sums, up_sums, half_all, mate_half, own_squares, square_slots,
    part_send, part_recv, land_send, land_recv, ring_send, ring_recv, z_send, z_recv,
    pair_send, pair_recv, y_send, y_recv, x_send, x_recv, pass_send, pass_recv, col_send, col_recv,
):
    r, c, p = lax.axis_index("row"), lax.axis_index("col"), lax.axis_index("rep")
    x_at, y_at = c // 4, c % 4
    mate = (r, c, 1 - p)
    sides = {
        "x": ((r, ((x_at + 3) % 4) * 4 + y_at, p), (r, ((x_at + 1) % 4) * 4 + y_at, p)),
        "y": ((r, x_at * 4 + (y_at + 3) % 4, p), (r, x_at * 4 + (y_at + 1) % 4, p)),
    }
    where = {"x": x_at, "y": y_at}
    alone = (c // 8 == p) & (c % 2 == p)

    def peer(step):
        return (r, (c + step) % 16, p)

    def level(step):
        return ((r + step) % 8, c, p)

    first = c // 2
    fetched = {}
    for q in range(2):
        for step in range(8):
            cols = pl.ds(pl.multiple_of(512 * (2 * ((first + step) % 8) + p), 512), 512)
            fetched[q, step] = pltpu.make_async_copy(
                slab.at[0, pl.ds(32 * q, 32), cols], own_blocks.at[q, step], block_sem.at[q, step]
            )
            fetched[q, step].start()
    basis_copy = pltpu.make_async_copy(basis_in, basis, in_sem.at[0])
    basis_copy.start()
    momentum_copy = pltpu.make_async_copy(momentum_in, momentum, in_sem.at[1])
    momentum_copy.start()

    barrier = pltpu.get_barrier_semaphore()
    pl.semaphore_signal(barrier, inc=1, device_id=mate, device_id_type=MESH)
    for step in range(1, 16):
        pl.semaphore_signal(barrier, inc=1, device_id=peer(step), device_id_type=MESH)
    for step in range(1, 8):
        pl.semaphore_signal(barrier, inc=1, device_id=level(step), device_id_type=MESH)
    for slot in range(8):
        @pl.when(jnp.logical_not(alone & (8 * p + slot == c)))
        def _():
            pl.semaphore_signal(barrier, inc=1, device_id=(r, 8 * p + slot, c % 2), device_id_type=MESH)
    pl.semaphore_wait(barrier, jnp.where(alone, 30, 31))

    started = []

    copies = {}
    for q in range(2):
        for step in range(8):
            b = (first + step) % 8
            cols = pl.ds(pl.multiple_of(512 * (2 * b + 1 - p), 512), 512)
            copy = remote(
                slab.at[0, pl.ds(32 * q, 32), cols], part.at[q, step], part_send.at[q, step], part_recv.at[q, step], mate
            )
            copy.start()
            copies[q, step] = copy
            started.append(copy)

    def block_copy(q, step):
        d = 2 * ((first + step) % 8) + p
        own = (d == c) & (c // 8 == p)
        slot = c % 8
        return own, remote(
            total.at[q, step], landed.at[q, slot], land_send.at[q, step], land_recv.at[q, slot], (r, d, c // 8)
        )

    for q in range(2):
        for step in range(8):
            copies[q, step].wait_recv()
            fetched[q, step].wait()
            total[q, step] = part[q, step] + own_blocks[q, step]
            own, copy = block_copy(q, step)

            @pl.when(own)
            def _():
                landed[q, c % 8] = total[q, step]

            @pl.when(jnp.logical_not(own))
            def _():
                copy.start()

    basis_copy.wait()
    momentum_copy.wait()
    high, low = split(basis[...])
    basis_high[...] = high
    basis_low[...] = low

    def land(q):
        for slot in range(8):
            @pl.when(jnp.logical_not(alone & (8 * p + slot == c)))
            def _():
                remote(
                    total.at[q, 0], landed.at[q, slot], land_send.at[q, 0], land_recv.at[q, slot],
                    (r, 8 * p + slot, c % 2),
                ).wait_recv()
            rows = slice(64 * slot + 32 * q, 64 * slot + 32 * q + 32)
            buffer[rows, :] = momentum[rows, :] + landed[q, slot]
        tile = jnp.concatenate([buffer[64 * s + 32 * q : 64 * s + 32 * q + 32, :] for s in range(8)], axis=0)
        tile = split(tile)
        for h in range(2):
            cols = slice(512 * h, 512 * h + 512)
            got = dot3(tile, (basis_high[:, cols], basis_low[:, cols]), ((1,), (0,)))
            for u in range(4):
                for v in range(4):
                    n = 4 * u + v
                    f, s = (u, v) if h == 0 else (v, u)
                    panel[q, h, f, s] = got[16 * n : 16 * n + 16]

    line = {
        "x": lambda step: (r, 4 * ((x_at + step) % 4) + y_at, p),
        "y": lambda step: (r, 4 * x_at + (y_at + step) % 4, p),
    }

    def direct_sum(piece, out, slots, pos, device, send, recv):
        moves = []
        for step in range(1, 4):
            move = remote(piece((pos + step) % 4), slots.at[step - 1], send.at[1, step], recv.at[1, step], device(step))
            move.start()
            moves.append(move)
        yield
        for move in moves:
            move.wait_recv()
        own = out(pos)
        own[...] = piece(pos)[...] + (slots[0] + slots[1] + slots[2])
        for step in range(1, 4):
            move = remote(own, own, send.at[2, step], recv.at[2, step], device(step))
            move.start()
            moves.append(move)
        yield
        for move in moves[3:]:
            move.wait_recv()
        started.extend(moves)

    def total_over_col(q, h):
        axis, other = ("x", "y") if h == 0 else ("y", "x")
        f, s = where[axis], where[other]
        yield from ring_scatter(
            lambda i: panel.at[q, h, i],
            lambda i, k: panel.at[q, h, i, pl.ds(2 * k, 2)],
            from_a.at[q, h], from_b.at[q, h], from_left.at[q, h], from_right.at[q, h],
            f, *sides[axis], ring_send.at[q, h, 0], ring_recv.at[q, h, 0], started,
        )
        yield from direct_sum(
            lambda i: panel.at[q, h, f, i], lambda i: full.at[q, h, f, i], others.at[q, h],
            s, line[other], ring_send.at[q, h], ring_recv.at[q, h],
        )
        yield
        yield from ring_gather(
            lambda i: full.at[q, h, i],
            lambda i, k: full.at[q, h, i, pl.ds(2 * k, 2)],
            f, *sides[axis], ring_send.at[q, h, 3], ring_recv.at[q, h, 3], started,
        )

    sums = {(q, h): total_over_col(q, h) for q in range(2) for h in range(2)}
    for q in range(2):
        land(q)
        for h in range(2):
            next(sums[q, h])
    out_copies = [pltpu.make_async_copy(buffer, buffer_out, out_sem.at[0])]
    out_copies[0].start()
    lockstep(sums[0, 0], sums[0, 1], sums[1, 0], sums[1, 1])
    for q in range(2):
        for u in range(4):
            for v in range(4):
                n = 4 * u + v
                top = 64 * (n // 2) + 32 * q + 16 * (n % 2)
                left_panel[top : top + 16, 0:512] = full[q, 0, u, v]
                left_panel[top : top + 16, 512:1024] = full[q, 1, v, u]

    column = pl.ds(pl.multiple_of(NB * (c // 2), NB), NB)
    left_split = split(left_panel[...])
    left_high[...] = left_split[0]
    left_low[...] = left_split[1]
    gram_part[...] = dot3(left_split, split(left_panel[:, column]), ((0,), (0,)))
    for q in range(2):
        for b in range(8):
            rows = pl.ds(pl.multiple_of(NB * b + 64 * (c % 2) + 32 * q, 32), 32)
            gram_pieces[q, b] = gram_part[rows, :]
    swap = remote(gram_pieces.at[1 - p], gram_in, pair_send.at[0], pair_recv.at[0], mate)
    swap.start()
    started.append(swap)

    def cross(q):
        cross_part[q] = dot3(split(buffer[:, 256 * q : 256 * q + 256]), left_split, ((0,), (0,)))

    swap.wait_recv()
    gram_pieces[p] = gram_pieces[p] + gram_in[...]
    moves = []
    for step in range(1, 8):
        z = (r + step) % 8
        move = remote(gram_pieces.at[p, z], gram_slots.at[r], z_send.at[0, step], z_recv.at[0, step], level(step))
        move.start()
        moves.append(move)
    started += moves
    gram_slots[r] = gram_pieces[p, r]
    cross(0)
    for move in moves:
        move.wait_recv()
    acc = gram_slots[0]
    for z in range(1, 8):
        acc = acc + gram_slots[z]
    gram_all[p, r, x_at, y_at] = acc
    moves = []
    for step in range(1, 8):
        own = gram_all.at[p, r, x_at, y_at]
        move = remote(own, own, z_send.at[1, step], z_recv.at[1, step], level(step))
        move.start()
        moves.append(move)
    started += moves
    cross(1)
    cross_swap = remote(cross_part.at[1 - p], cross_in, pair_send.at[1], pair_recv.at[1], mate)
    cross_swap.start()
    started.append(cross_swap)
    for move in moves:
        move.wait_recv()

    direct = (0, 1)

    def along_y(part, step):
        own = gram_all.at[p, pl.ds(part, 1 + 6 * part), x_at, y_at]
        device = (r, 4 * x_at + (y_at + step) % 4, p)
        return remote(own, own, y_send.at[part, step], y_recv.at[part, step], device)

    def along_x(b, step, other=0):
        own = gram_all.at[p, b, x_at]
        device = (r, 4 * ((x_at + step) % 4) + y_at, (p + other) % 2)
        index = 8 * other + b
        return remote(own, own, x_send.at[index, step], x_recv.at[index, step], device)

    def x_start(b):
        @pl.when(2 * x_at + 1 >= b)
        def _():
            for step in range(1, 4):
                along_x(b, step).start()
            if b in direct:
                for step in range(4):
                    along_x(b, step, 1).start()

    def x_wait(b):
        for step in range(1, 4):
            @pl.when(2 * ((x_at + 4 - step) % 4) + 1 >= b)
            def _():
                along_x(b, step).wait_recv()
        if b in direct:
            for step in range(4):
                along_x(b, step, 1).wait_recv()

    passed = {}

    def x_pass(b):
        view = gram_all.at[p, b, pl.ds(b // 2, 4 - b // 2)]
        passed[b] = remote(view, view, pass_send.at[b], pass_recv.at[b], mate)
        passed[b].start()
        started.append(passed[b])

    def rows_of(z):
        return pl.ds(pl.multiple_of(32 * z, 32), 32)

    for part in range(2):
        for step in range(1, 4):
            along_y(part, step).start()
    for step in range(1, 4):
        along_y(0, step).wait_recv()
    x_start(0)
    for step in range(1, 4):
        along_y(1, step).wait_recv()
    x_start(1)
    x_start(2)
    lower, upper = level(7), level(1)
    handed = []

    def hand(z):
        rows = rows_of(z)
        copy = remote(half_all.at[rows], mate_half.at[rows], pass_send.at[8 + len(handed)], pass_recv.at[8 + len(handed)], mate)
        copy.start()
        handed.append(copy)
        started.append(copy)

    def row_piece(offset):
        return cross_part.at[p, rows_of((r + 8 + offset) % 8)]

    def hop(src, dst, index, device):
        copy = remote(src, dst, z_send.at[2 + index // 8, index % 8], z_recv.at[2 + index // 8, index % 8], device)
        copy.start()
        started.append(copy)
        return copy

    def cross_sum():
        cross_swap.wait_recv()
        cross_part[p] = cross_part[p] + cross_in[...]
        a = hop(row_piece(-4), down_sums.at[0], 0, lower)
        yield
        a.wait_recv()
        down_sums[0] = down_sums[0] + row_piece(-3)[...]
        a = hop(down_sums.at[0], down_sums.at[1], 1, lower)
        b = hop(row_piece(3), up_sums.at[0], 4, upper)
        yield
        for step in (1, 2):
            a.wait_recv()
            down_sums[step] = down_sums[step] + row_piece(step - 3)[...]
            a = hop(down_sums.at[step], down_sums.at[step + 1], 1 + step, lower)
            b.wait_recv()
            up_sums[step - 1] = up_sums[step - 1] + row_piece(3 - step)[...]
            b = hop(up_sums.at[step - 1], up_sums.at[step], 4 + step, upper)
            yield
        a.wait_recv()
        b.wait_recv()
        own = half_all.at[rows_of(r)]
        own[...] = row_piece(0)[...] + (down_sums[3] + up_sums[2])
        a = hop(own, own, 8, lower)
        b = hop(own, own, 9, upper)
        hand(r)
        yield
        for step in (1, 2, 3):
            a.wait_recv()
            view = half_all.at[rows_of((r + step) % 8)]
            a = hop(view, view, 8 + 2 * step, lower)
            b.wait_recv()
            if step < 3:
                view = half_all.at[rows_of((r + 8 - step) % 8)]
                b = hop(view, view, 9 + 2 * step, upper)
            hand((r + step) % 8)
            hand((r + 8 - step) % 8)
            yield
        a.wait_recv()
        hand((r + 4) % 8)
        yield

    corner_rows = lax.broadcasted_iota(jnp.int32, (256, 256), 0)
    corner_cols = lax.broadcasted_iota(jnp.int32, (256, 256), 1)

    def solve_band(high, low, out, at, j):
        n = 256 * j + 256
        band = x[256 * j : n, :n]
        corner = jnp.where(corner_rows >= corner_cols, band[:, 256 * j :], 0.0)
        band = split(jnp.concatenate([band[:, : 256 * j], corner], axis=1) if j else corner)
        out[at, 256 * j : n] = dot3((high[:, :n], low[:, :n]), band, ((1,), (1,)))

    def solve(panel, out, at):
        high, low = split(panel)
        for j in range(4):
            solve_band(high, low, out, at, j)

    crossing = cross_sum()
    next(crossing)
    for k in range(8):
        if k in direct:
            x_wait(k)
        else:
            passed[k].wait_recv()
        if k + 1 < 8 and k + 1 not in direct:
            x_wait(k + 1)
            x_pass(k + 1)
        if k + 3 < 8:
            x_start(k + 3)
        next(crossing)
        place_rows(x, gram_all, k)
        chol_step(x, k)
        if k in (2, 4, 6):
            solve_band(left_high, left_low, left_unit, slice(0, 512), k // 2 - 1)

    for copy in handed:
        copy.wait_recv()
    for q in range(2):
        @pl.when(p == q)
        def _():
            solve(half_all[...], right_panel, slice(256 * q, 256 * q + 256))
            solve(mate_half[...], right_panel, slice(256 - 256 * q, 512 - 256 * q))
    out_copies.append(pltpu.make_async_copy(right_panel, panel_out, out_sem.at[1]))
    out_copies[1].start()
    v = right_panel[...]
    square_sums = jnp.sum(v * v, axis=0, keepdims=True)
    for k in range(8):
        own_squares[k : k + 1, :] = square_sums[:, 128 * k : 128 * k + 128]
    square_slots[c] = own_squares[...]
    moves = []
    for step in range(1, 16):
        move = remote(own_squares, square_slots.at[c], col_send.at[step], col_recv.at[step], peer(step))
        move.start()
        moves.append(move)
    started += moves
    solve_band(left_high, left_low, left_unit, slice(0, 512), 3)
    unit = split(left_unit[...])
    inner[...] = dot3(unit, split(right_panel[...]), ((1,), (1,)))
    out_copies.append(pltpu.make_async_copy(inner, inner_out, out_sem.at[2]))
    out_copies[2].start()
    for move in moves:
        move.wait_recv()
    acc = square_slots[0]
    for i in range(1, 16):
        acc = acc + square_slots[i]
    norms = jnp.sqrt(acc + EPSILON)
    for k in range(8):
        norm[:, 128 * k : 128 * k + 128] = norms[k : k + 1, :]
    scaled[...] = dot3(unit, split(right_panel[...] / norm[...]), ((1,), (1,)))

    for copy in out_copies:
        copy.wait()
    for move in started:
        move.wait_send()
    for q in range(2):
        for step in range(8):
            own, copy = block_copy(q, step)

            @pl.when(jnp.logical_not(own))
            def _():
                copy.wait_send()
    for part in range(2):
        for step in range(1, 4):
            along_y(part, step).wait_send()
    for b in range(8):
        @pl.when(2 * x_at + 1 >= b)
        def _():
            for step in range(1, 4):
                along_x(b, step).wait_send()
            if b in direct:
                for step in range(4):
                    along_x(b, step, 1).wait_send()


def panels(gradients, momentum, right_basis):
    f32 = jnp.float32
    vmem = pl.BlockSpec(memory_space=pltpu.VMEM)
    anywhere = pl.BlockSpec(memory_space=pl.ANY)
    dma = pltpu.SemaphoreType.DMA
    return pl.pallas_call(
        main_kernel,
        out_shape=[
            jax.ShapeDtypeStruct((512, 512), f32),
            jax.ShapeDtypeStruct((512, N), f32),
            jax.ShapeDtypeStruct((1, N), f32),
            jax.ShapeDtypeStruct((512, 512), f32),
            jax.ShapeDtypeStruct((512, 512), f32),
        ],
        in_specs=[anywhere] * 3,
        out_specs=[anywhere, anywhere, vmem, anywhere, vmem],
        scratch_shapes=[
            pltpu.VMEM((512, 512), f32),
            pltpu.VMEM((512, N), f32),
            pltpu.VMEM((2, 8, 32, 512), f32),
            pltpu.VMEM((512, 512), f32),
            pltpu.VMEM((512, N), f32),
            pltpu.VMEM((512, 512), f32),
            dma((2,)), dma((2, 8)), dma((3,)),
            pltpu.VMEM((512, N), f32),
            pltpu.VMEM((2, 8, 32, 512), f32),
            pltpu.VMEM((2, 8, 32, 512), f32),
            pltpu.VMEM((2, 8, 32, 512), f32),
            pltpu.VMEM((512, N), jnp.bfloat16),
            pltpu.VMEM((512, N), jnp.bfloat16),
            pltpu.VMEM((2, 2, 4, 4, 16, 512), f32),
            pltpu.VMEM((2, 2, 2, 16, 512), f32),
            pltpu.VMEM((2, 2, 2, 16, 512), f32),
            pltpu.VMEM((2, 2, 4, 16, 512), f32),
            pltpu.VMEM((2, 2, 4, 16, 512), f32),
            pltpu.VMEM((2, 2, 3, 16, 512), f32),
            pltpu.VMEM((2, 2, 4, 4, 16, 512), f32),
            pltpu.VMEM((512, N), f32),
            pltpu.VMEM((512, N), jnp.bfloat16),
            pltpu.VMEM((512, N), jnp.bfloat16),
            pltpu.VMEM((N, NB), f32),
            pltpu.VMEM((2, 8, 32, NB), f32),
            pltpu.VMEM((8, 32, NB), f32),
            pltpu.VMEM((8, 32, NB), f32),
            pltpu.VMEM((2, 8, 4, 4, 32, NB), f32),
            pltpu.VMEM((N, N), f32),
            pltpu.VMEM((2, 256, N), f32),
            pltpu.VMEM((256, N), f32),
            pltpu.VMEM((4, 32, N), f32),
            pltpu.VMEM((3, 32, N), f32),
            pltpu.VMEM((256, N), f32),
            pltpu.VMEM((256, N), f32),
            pltpu.VMEM((8, 128), f32),
            pltpu.VMEM((16, 8, 128), f32),
            dma((2, 8)), dma((2, 8)), dma((2, 8)), dma((2, 8)),
            dma((2, 2, 4, 4)), dma((2, 2, 4, 4)),
            dma((4, 8)), dma((4, 8)),
            dma((2,)), dma((2,)),
            dma((2, 4)), dma((2, 4)),
            dma((16, 4)), dma((16, 4)),
            dma((16,)), dma((16,)),
            dma((16,)), dma((16,)),
        ],
        compiler_params=pltpu.CompilerParams(collective_id=0, has_side_effects=True, vmem_limit_bytes=56 << 20),
    )(gradients, momentum, right_basis)


def shards(gradients, momentum, right_basis):
    buffer, right_panel, norm, inner, scaled = panels(gradients, momentum, right_basis)
    new_basis = right_panel / norm
    new_momentum = buffer - (1.0 - DECAY) * inner
    update = (D / math.sqrt(N)) * scaled
    return (new_momentum, new_basis, update)


def solution(mesh):
    return jax.shard_map(
        shards,
        mesh=mesh,
        in_specs=(P("rep", ("row", "col"), None), P(("row", "rep"), "col"), P("col", None)),
        out_specs=(P(("row", "rep"), "col"), P("col", None), P(("row", "rep"), "col")),
        check_vma=False,
    )
```

```python
import functools
import math

import jax
import jax.numpy as jnp
from jax import lax
from jax.experimental import pallas as pl
from jax.experimental.pallas import tpu as pltpu
from jax.sharding import PartitionSpec as P

N = 1024
NB = 128
HI = lax.Precision.HIGHEST
EPSILON = 1e-06
RIDGE = 0.001
DECAY = 0.95
D = 8192
MESH = pl.DeviceIdType.MESH


def dot(left, right, dims, precision=HI):
    return lax.dot_general(left, right, (dims, ((), ())), precision=precision, preferred_element_type=jnp.float32)


def split(a):
    high = a.astype(jnp.bfloat16)
    return high, (a - high.astype(jnp.float32)).astype(jnp.bfloat16)


def dot3(left, right, dims):
    def one(a, b):
        return lax.dot_general(a, b, (dims, ((), ())), preferred_element_type=jnp.float32)

    return one(left[0], right[0]) + (one(left[0], right[1]) + one(left[1], right[0]))


def factor_block(rest):
    lane = lax.broadcasted_iota(jnp.int32, (8, NB), 1)
    sub = lax.broadcasted_iota(jnp.int32, (8, NB), 0)
    done = []
    for base in range(0, NB, 8):
        top, rest = rest[:8], rest[8:]
        n = rest.shape[0]
        inside = (lane >= base) & (lane < base + 8)
        pivots = [jnp.broadcast_to(top[:, base + k : base + k + 1], (8, NB)) for k in range(8)]
        top = jnp.where(inside, jnp.where(lane - base == sub, 1.0, 0.0), top)
        if n:
            below = [jnp.broadcast_to(rest[:, base + k : base + k + 1], (n, NB)) for k in range(8)]
            wide = lax.broadcasted_iota(jnp.int32, (n, NB), 1)
            rest = jnp.where((wide >= base) & (wide < base + 8), 0.0, rest)
        for k in range(8):
            scale = lax.rsqrt(pivots[k][k : k + 1, :])
            row = top[k : k + 1, :] * scale
            factor = jnp.where(sub > k, pivots[k] * scale, 0.0)
            top = jnp.where(sub == k, row, top - factor * row)
            cross = {}
            for q in range(k + 1, 8):
                cross[q] = pivots[q][k : k + 1, :] * scale
                pivots[q] = pivots[q] - factor * cross[q]
            if n:
                lower = below[k] * scale
                rest = rest - lower * row
                for q in range(k + 1, 8):
                    below[q] = below[q] - lower * cross[q]
        done.append(top)
    return jnp.concatenate(done, axis=0)


def remote(src, dst, send, recv, device):
    return pltpu.make_async_remote_copy(
        src_ref=src, dst_ref=dst, send_sem=send, recv_sem=recv, device_id=device, device_id_type=MESH
    )


def ring_scatter(piece, half, from_a, from_b, from_left, from_right, pos, left, right, send, recv, started):
    before, after, across = (pos + 3) % 4, (pos + 1) % 4, (pos + 2) % 4
    a = remote(half(across, 0), from_a, send.at[0], recv.at[0], left)
    b = remote(half(across, 1), from_b, send.at[1], recv.at[1], right)
    a.start()
    b.start()
    yield
    a.wait_recv()
    half(before, 0)[...] = half(before, 0)[...] + from_a[...]
    c = remote(piece(before), from_right, send.at[2], recv.at[2], left)
    c.start()
    b.wait_recv()
    half(after, 1)[...] = half(after, 1)[...] + from_b[...]
    d = remote(piece(after), from_left, send.at[3], recv.at[3], right)
    d.start()
    yield
    c.wait_recv()
    d.wait_recv()
    piece(pos)[...] = piece(pos)[...] + (from_left[...] + from_right[...])
    started += [a, b, c, d]


def ring_gather(piece, half, pos, left, right, send, recv, started, done=None):
    before, after, across = (pos + 3) % 4, (pos + 1) % 4, (pos + 2) % 4
    a = remote(piece(pos), piece(pos), send.at[0], recv.at[0], left)
    b = remote(piece(pos), piece(pos), send.at[1], recv.at[1], right)
    a.start()
    b.start()
    if done:
        done(0, pos)
    yield
    a.wait_recv()
    c = remote(half(after, 0), half(after, 0), send.at[2], recv.at[2], left)
    c.start()
    b.wait_recv()
    d = remote(half(before, 1), half(before, 1), send.at[3], recv.at[3], right)
    d.start()
    if done:
        done(1, after)
        done(2, before)
    yield
    c.wait_recv()
    d.wait_recv()
    if done:
        done(3, across)
    started += [a, b, c, d]


def lockstep(*stages):
    stages = list(stages)
    while stages:
        for stage in list(stages):
            try:
                next(stage)
            except StopIteration:
                stages.remove(stage)


def place_rows(x, gram_all, k):
    rows = slice(NB * k, NB * k + NB)
    for j in range(k, N // NB):
        parts = [gram_all[p, k, j // 2, 2 * (j % 2) + h] for h in range(2) for p in range(2)]
        block = jnp.concatenate(parts, axis=0)
        cols = slice(NB * j, NB * j + NB)
        x[rows, cols] = block if k == 0 else x[rows, cols] + block


def chol_step(x, k):
    r = lax.broadcasted_iota(jnp.int32, (NB, NB), 0)
    c = lax.broadcasted_iota(jnp.int32, (NB, NB), 1)
    a, b = NB * k, NB * k + NB
    block = factor_block(x[a:b, a:b] + jnp.where(r == c, RIDGE, 0.0))
    low = jnp.where(r >= c, block, 0.0)
    x[a:b, a:b] = low
    low = split(low)
    done, ahead = low, None
    if a:
        left = dot3(low, split(x[a:b, :a]), ((1,), (0,)))
        x[a:b, :a] = left
        done = [jnp.concatenate(pair, axis=1) for pair in zip(split(left), low)]
    if b < N:
        right = dot3(low, split(x[a:b, b:]), ((1,), (0,)))
        x[a:b, b:] = right
        ahead = split(right)
    for i in range(b, N, NB):
        factor = [half[:, i - b : i - b + NB] for half in ahead]
        left = dot3(factor, done, ((0,), (0,)))
        right = dot3(factor, [half[:, i - b :] for half in ahead], ((0,), (0,)))
        x[i : i + NB, a:b] = -left[:, a:]
        if a:
            x[i : i + NB, :a] = x[i : i + NB, :a] - left[:, :a]
            x[i : i + NB, i:] = x[i : i + NB, i:] - right
        else:
            x[i : i + NB, i:] = -right


def main_kernel(
    slab, momentum_in, basis_in,
    buffer_out, panel_out, norm, inner_out, scaled,
    momentum, basis, own_blocks, buffer, right_panel, in_sem, block_sem, out_sem,
    part, total, landed, basis_high, basis_low, panel, from_a, from_b, from_left, from_right,
    others, full, left_panel, left_high, left_low,
    gram_part, gram_pieces, gram_in, gram_slots, gram_all, x,
    cross_part, cross_in, down_sums, up_sums, half_all, mate_half, own_squares, square_slots,
    part_send, part_recv, land_send, land_recv, ring_send, ring_recv, z_send, z_recv,
    pair_send, pair_recv, y_send, y_recv, x_send, x_recv, pass_send, pass_recv, col_send, col_recv,
):
    r, c, p = lax.axis_index("row"), lax.axis_index("col"), lax.axis_index("rep")
    x_at, y_at = c // 4, c % 4
    mate = (r, c, 1 - p)
    sides = {
        "x": ((r, ((x_at + 3) % 4) * 4 + y_at, p), (r, ((x_at + 1) % 4) * 4 + y_at, p)),
        "y": ((r, x_at * 4 + (y_at + 3) % 4, p), (r, x_at * 4 + (y_at + 1) % 4, p)),
    }
    where = {"x": x_at, "y": y_at}
    alone = (c // 8 == p) & (c % 2 == p)

    def peer(step):
        return (r, (c + step) % 16, p)

    def level(step):
        return ((r + step) % 8, c, p)

    left_unit, inner = basis, momentum

    first = c // 2
    fetched = {}
    for q in range(2):
        for step in range(8):
            cols = pl.ds(pl.multiple_of(512 * (2 * ((first + step) % 8) + p), 512), 512)
            fetched[q, step] = pltpu.make_async_copy(
                slab.at[0, pl.ds(32 * q, 32), cols], own_blocks.at[q, step], block_sem.at[q, step]
            )
            fetched[q, step].start()
    basis_copy = pltpu.make_async_copy(basis_in, basis, in_sem.at[0])
    basis_copy.start()
    momentum_copy = pltpu.make_async_copy(momentum_in, momentum, in_sem.at[1])
    momentum_copy.start()

    barrier = pltpu.get_barrier_semaphore()
    pl.semaphore_signal(barrier, inc=1, device_id=mate, device_id_type=MESH)
    for step in range(1, 16):
        pl.semaphore_signal(barrier, inc=1, device_id=peer(step), device_id_type=MESH)
    for step in range(1, 8):
        pl.semaphore_signal(barrier, inc=1, device_id=level(step), device_id_type=MESH)
    for slot in range(8):
        @pl.when(jnp.logical_not(alone & (8 * p + slot == c)))
        def _():
            pl.semaphore_signal(barrier, inc=1, device_id=(r, 8 * p + slot, c % 2), device_id_type=MESH)
    pl.semaphore_wait(barrier, jnp.where(alone, 30, 31))

    started = []

    copies = {}
    for q in range(2):
        for step in range(8):
            b = (first + step) % 8
            cols = pl.ds(pl.multiple_of(512 * (2 * b + 1 - p), 512), 512)
            copy = remote(
                slab.at[0, pl.ds(32 * q, 32), cols], part.at[q, step], part_send.at[q, step], part_recv.at[q, step], mate
            )
            copy.start()
            copies[q, step] = copy
            started.append(copy)

    def block_copy(q, step):
        d = 2 * ((first + step) % 8) + p
        own = (d == c) & (c // 8 == p)
        slot = c % 8
        return own, remote(
            total.at[q, step], landed.at[q, slot], land_send.at[q, step], land_recv.at[q, slot], (r, d, c // 8)
        )

    for q in range(2):
        for step in range(8):
            copies[q, step].wait_recv()
            fetched[q, step].wait()
            total[q, step] = part[q, step] + own_blocks[q, step]
            own, copy = block_copy(q, step)

            @pl.when(own)
            def _():
                landed[q, c % 8] = total[q, step]

            @pl.when(jnp.logical_not(own))
            def _():
                copy.start()

    basis_copy.wait()
    momentum_copy.wait()
    high, low = split(basis[...])
    basis_high[...] = high
    basis_low[...] = low

    def land(q):
        for slot in range(8):
            @pl.when(jnp.logical_not(alone & (8 * p + slot == c)))
            def _():
                remote(
                    total.at[q, 0], landed.at[q, slot], land_send.at[q, 0], land_recv.at[q, slot],
                    (r, 8 * p + slot, c % 2),
                ).wait_recv()
            rows = slice(64 * slot + 32 * q, 64 * slot + 32 * q + 32)
            buffer[rows, :] = momentum[rows, :] + landed[q, slot]
        tile = jnp.concatenate([buffer[64 * s + 32 * q : 64 * s + 32 * q + 32, :] for s in range(8)], axis=0)
        tile = split(tile)
        for h in range(2):
            cols = slice(512 * h, 512 * h + 512)
            got = dot3(tile, (basis_high[:, cols], basis_low[:, cols]), ((1,), (0,)))
            for u in range(4):
                for v in range(4):
                    n = 4 * u + v
                    f, s = (u, v) if h == 0 else (v, u)
                    panel[q, h, f, s] = got[16 * n : 16 * n + 16]

    line = {
        "x": lambda step: (r, 4 * ((x_at + step) % 4) + y_at, p),
        "y": lambda step: (r, 4 * x_at + (y_at + step) % 4, p),
    }

    def direct_sum(piece, out, slots, pos, device, send, recv):
        moves = []
        for step in range(1, 4):
            move = remote(piece((pos + step) % 4), slots.at[step - 1], send.at[1, step], recv.at[1, step], device(step))
            move.start()
            moves.append(move)
        yield
        for move in moves:
            move.wait_recv()
        own = out(pos)
        own[...] = piece(pos)[...] + (slots[0] + slots[1] + slots[2])
        for step in range(1, 4):
            move = remote(own, own, send.at[2, step], recv.at[2, step], device(step))
            move.start()
            moves.append(move)
        yield
        for move in moves[3:]:
            move.wait_recv()
        started.extend(moves)

    def total_over_col(q, h):
        axis, other = ("x", "y") if h == 0 else ("y", "x")
        f, s = where[axis], where[other]
        yield from ring_scatter(
            lambda i: panel.at[q, h, i],
            lambda i, k: panel.at[q, h, i, pl.ds(2 * k, 2)],
            from_a.at[q, h], from_b.at[q, h], from_left.at[q, h], from_right.at[q, h],
            f, *sides[axis], ring_send.at[q, h, 0], ring_recv.at[q, h, 0], started,
        )
        yield from direct_sum(
            lambda i: panel.at[q, h, f, i], lambda i: full.at[q, h, f, i], others.at[q, h],
            s, line[other], ring_send.at[q, h], ring_recv.at[q, h],
        )
        yield
        yield from ring_gather(
            lambda i: full.at[q, h, i],
            lambda i, k: full.at[q, h, i, pl.ds(2 * k, 2)],
            f, *sides[axis], ring_send.at[q, h, 3], ring_recv.at[q, h, 3], started,
        )

    sums = {(q, h): total_over_col(q, h) for q in range(2) for h in range(2)}
    for q in range(2):
        land(q)
        for h in range(2):
            next(sums[q, h])
    out_copies = [pltpu.make_async_copy(buffer, buffer_out, out_sem.at[0])]
    out_copies[0].start()
    lockstep(sums[0, 0], sums[0, 1], sums[1, 0], sums[1, 1])
    for q in range(2):
        for u in range(4):
            for v in range(4):
                n = 4 * u + v
                top = 64 * (n // 2) + 32 * q + 16 * (n % 2)
                left_panel[top : top + 16, 0:512] = full[q, 0, u, v]
                left_panel[top : top + 16, 512:1024] = full[q, 1, v, u]

    column = pl.ds(pl.multiple_of(NB * (c // 2), NB), NB)
    left_split = split(left_panel[...])
    left_high[...] = left_split[0]
    left_low[...] = left_split[1]
    gram_part[...] = dot3(left_split, split(left_panel[:, column]), ((0,), (0,)))
    for q in range(2):
        for b in range(8):
            rows = pl.ds(pl.multiple_of(NB * b + 64 * (c % 2) + 32 * q, 32), 32)
            gram_pieces[q, b] = gram_part[rows, :]
    swap = remote(gram_pieces.at[1 - p], gram_in, pair_send.at[0], pair_recv.at[0], mate)
    swap.start()
    started.append(swap)

    def cross(q):
        cross_part[q] = dot3(split(buffer[:, 256 * q : 256 * q + 256]), left_split, ((0,), (0,)))

    swap.wait_recv()
    gram_pieces[p] = gram_pieces[p] + gram_in[...]
    moves = []
    for step in range(1, 8):
        z = (r + step) % 8
        move = remote(gram_pieces.at[p, z], gram_slots.at[r], z_send.at[0, step], z_recv.at[0, step], level(step))
        move.start()
        moves.append(move)
    started += moves
    gram_slots[r] = gram_pieces[p, r]
    cross(0)
    for move in moves:
        move.wait_recv()
    acc = gram_slots[0]
    for z in range(1, 8):
        acc = acc + gram_slots[z]
    gram_all[p, r, x_at, y_at] = acc
    moves = []
    for step in range(1, 8):
        own = gram_all.at[p, r, x_at, y_at]
        move = remote(own, own, z_send.at[1, step], z_recv.at[1, step], level(step))
        move.start()
        moves.append(move)
    started += moves
    cross(1)
    cross_swap = remote(cross_part.at[1 - p], cross_in, pair_send.at[1], pair_recv.at[1], mate)
    cross_swap.start()
    started.append(cross_swap)
    for move in moves:
        move.wait_recv()

    direct = (0, 1)

    def along_y(part, step):
        own = gram_all.at[p, pl.ds(part, 1 + 6 * part), x_at, y_at]
        device = (r, 4 * x_at + (y_at + step) % 4, p)
        return remote(own, own, y_send.at[part, step], y_recv.at[part, step], device)

    def along_x(b, step, other=0):
        own = gram_all.at[p, b, x_at]
        device = (r, 4 * ((x_at + step) % 4) + y_at, (p + other) % 2)
        index = 8 * other + b
        return remote(own, own, x_send.at[index, step], x_recv.at[index, step], device)

    def x_start(b):
        @pl.when(2 * x_at + 1 >= b)
        def _():
            for step in range(1, 4):
                along_x(b, step).start()
            if b in direct:
                for step in range(4):
                    along_x(b, step, 1).start()

    def x_wait(b):
        for step in range(1, 4):
            @pl.when(2 * ((x_at + 4 - step) % 4) + 1 >= b)
            def _():
                along_x(b, step).wait_recv()
        if b in direct:
            for step in range(4):
                along_x(b, step, 1).wait_recv()

    passed = {}

    def x_pass(b):
        view = gram_all.at[p, b, pl.ds(b // 2, 4 - b // 2)]
        passed[b] = remote(view, view, pass_send.at[b], pass_recv.at[b], mate)
        passed[b].start()
        started.append(passed[b])

    def rows_of(z):
        return pl.ds(pl.multiple_of(32 * z, 32), 32)

    for part in range(2):
        for step in range(1, 4):
            along_y(part, step).start()
    for step in range(1, 4):
        along_y(0, step).wait_recv()
    x_start(0)
    for step in range(1, 4):
        along_y(1, step).wait_recv()
    x_start(1)
    x_start(2)
    lower, upper = level(7), level(1)
    handed = []

    def hand(z):
        rows = rows_of(z)
        copy = remote(half_all.at[rows], mate_half.at[rows], pass_send.at[8 + len(handed)], pass_recv.at[8 + len(handed)], mate)
        copy.start()
        handed.append(copy)
        started.append(copy)

    def row_piece(offset):
        return cross_part.at[p, rows_of((r + 8 + offset) % 8)]

    def hop(src, dst, index, device):
        copy = remote(src, dst, z_send.at[2 + index // 8, index % 8], z_recv.at[2 + index // 8, index % 8], device)
        copy.start()
        started.append(copy)
        return copy

    def cross_sum():
        cross_swap.wait_recv()
        cross_part[p] = cross_part[p] + cross_in[...]
        a = hop(row_piece(-4), down_sums.at[0], 0, lower)
        yield
        a.wait_recv()
        down_sums[0] = down_sums[0] + row_piece(-3)[...]
        a = hop(down_sums.at[0], down_sums.at[1], 1, lower)
        b = hop(row_piece(3), up_sums.at[0], 4, upper)
        yield
        for step in (1, 2):
            a.wait_recv()
            down_sums[step] = down_sums[step] + row_piece(step - 3)[...]
            a = hop(down_sums.at[step], down_sums.at[step + 1], 1 + step, lower)
            b.wait_recv()
            up_sums[step - 1] = up_sums[step - 1] + row_piece(3 - step)[...]
            b = hop(up_sums.at[step - 1], up_sums.at[step], 4 + step, upper)
            yield
        a.wait_recv()
        b.wait_recv()
        own = half_all.at[rows_of(r)]
        own[...] = row_piece(0)[...] + (down_sums[3] + up_sums[2])
        a = hop(own, own, 8, lower)
        b = hop(own, own, 9, upper)
        hand(r)
        yield
        for step in (1, 2, 3):
            a.wait_recv()
            view = half_all.at[rows_of((r + step) % 8)]
            a = hop(view, view, 8 + 2 * step, lower)
            b.wait_recv()
            if step < 3:
                view = half_all.at[rows_of((r + 8 - step) % 8)]
                b = hop(view, view, 9 + 2 * step, upper)
            hand((r + step) % 8)
            hand((r + 8 - step) % 8)
            yield
        a.wait_recv()
        hand((r + 4) % 8)
        yield

    corner_rows = lax.broadcasted_iota(jnp.int32, (256, 256), 0)
    corner_cols = lax.broadcasted_iota(jnp.int32, (256, 256), 1)

    def solve_band(high, low, out, at, j):
        n = 256 * j + 256
        band = x[256 * j : n, :n]
        corner = jnp.where(corner_rows >= corner_cols, band[:, 256 * j :], 0.0)
        band = split(jnp.concatenate([band[:, : 256 * j], corner], axis=1) if j else corner)
        out[at, 256 * j : n] = dot3((high[:, :n], low[:, :n]), band, ((1,), (1,)))

    def solve(panel, out, at):
        high, low = split(panel)
        for j in range(4):
            solve_band(high, low, out, at, j)

    crossing = cross_sum()
    next(crossing)
    for k in range(8):
        if k in direct:
            x_wait(k)
        else:
            passed[k].wait_recv()
        if k + 1 < 8 and k + 1 not in direct:
            x_wait(k + 1)
            x_pass(k + 1)
        if k + 3 < 8:
            x_start(k + 3)
        next(crossing)
        place_rows(x, gram_all, k)
        chol_step(x, k)
        if k in (2, 4, 6):
            solve_band(left_high, left_low, left_unit, slice(0, 512), k // 2 - 1)

    for copy in handed:
        copy.wait_recv()
    for q in range(2):
        @pl.when(p == q)
        def _():
            solve(half_all[...], right_panel, slice(256 * q, 256 * q + 256))
            solve(mate_half[...], right_panel, slice(256 - 256 * q, 512 - 256 * q))
    out_copies.append(pltpu.make_async_copy(right_panel, panel_out, out_sem.at[1]))
    out_copies[1].start()
    v = right_panel[...]
    square_sums = jnp.sum(v * v, axis=0, keepdims=True)
    for k in range(8):
        own_squares[k : k + 1, :] = square_sums[:, 128 * k : 128 * k + 128]
    square_slots[c] = own_squares[...]
    moves = []
    for step in range(1, 16):
        move = remote(own_squares, square_slots.at[c], col_send.at[step], col_recv.at[step], peer(step))
        move.start()
        moves.append(move)
    started += moves
    solve_band(left_high, left_low, left_unit, slice(0, 512), 3)
    unit = split(left_unit[...])
    inner[...] = dot3(unit, split(right_panel[...]), ((1,), (1,)))
    out_copies.append(pltpu.make_async_copy(inner, inner_out, out_sem.at[2]))
    out_copies[2].start()
    for move in moves:
        move.wait_recv()
    acc = square_slots[0]
    for i in range(1, 16):
        acc = acc + square_slots[i]
    norms = jnp.sqrt(acc + EPSILON)
    for k in range(8):
        norm[:, 128 * k : 128 * k + 128] = norms[k : k + 1, :]
    scaled[...] = dot3(unit, split(right_panel[...] / norm[...]), ((1,), (1,)))

    for copy in out_copies:
        copy.wait()
    for move in started:
        move.wait_send()
    for q in range(2):
        for step in range(8):
            own, copy = block_copy(q, step)

            @pl.when(jnp.logical_not(own))
            def _():
                copy.wait_send()
    for part in range(2):
        for step in range(1, 4):
            along_y(part, step).wait_send()
    for b in range(8):
        @pl.when(2 * x_at + 1 >= b)
        def _():
            for step in range(1, 4):
                along_x(b, step).wait_send()
            if b in direct:
                for step in range(4):
                    along_x(b, step, 1).wait_send()


def panels(gradients, momentum, right_basis):
    f32 = jnp.float32
    vmem = pl.BlockSpec(memory_space=pltpu.VMEM)
    anywhere = pl.BlockSpec(memory_space=pl.ANY)
    dma = pltpu.SemaphoreType.DMA
    return pl.pallas_call(
        main_kernel,
        out_shape=[
            jax.ShapeDtypeStruct((512, 512), f32),
            jax.ShapeDtypeStruct((512, N), f32),
            jax.ShapeDtypeStruct((1, N), f32),
            jax.ShapeDtypeStruct((512, 512), f32),
            jax.ShapeDtypeStruct((512, 512), f32),
        ],
        in_specs=[anywhere] * 3,
        out_specs=[anywhere, anywhere, vmem, anywhere, vmem],
        scratch_shapes=[
            pltpu.VMEM((512, 512), f32),
            pltpu.VMEM((512, N), f32),
            pltpu.VMEM((2, 8, 32, 512), f32),
            pltpu.VMEM((512, 512), f32),
            pltpu.VMEM((512, N), f32),
            dma((2,)), dma((2, 8)), dma((3,)),
            pltpu.VMEM((2, 8, 32, 512), f32),
            pltpu.VMEM((2, 8, 32, 512), f32),
            pltpu.VMEM((2, 8, 32, 512), f32),
            pltpu.VMEM((512, N), jnp.bfloat16),
            pltpu.VMEM((512, N), jnp.bfloat16),
            pltpu.VMEM((2, 2, 4, 4, 16, 512), f32),
            pltpu.VMEM((2, 2, 2, 16, 512), f32),
            pltpu.VMEM((2, 2, 2, 16, 512), f32),
            pltpu.VMEM((2, 2, 4, 16, 512), f32),
            pltpu.VMEM((2, 2, 4, 16, 512), f32),
            pltpu.VMEM((2, 2, 3, 16, 512), f32),
            pltpu.VMEM((2, 2, 4, 4, 16, 512), f32),
            pltpu.VMEM((512, N), f32),
            pltpu.VMEM((512, N), jnp.bfloat16),
            pltpu.VMEM((512, N), jnp.bfloat16),
            pltpu.VMEM((N, NB), f32),
            pltpu.VMEM((2, 8, 32, NB), f32),
            pltpu.VMEM((8, 32, NB), f32),
            pltpu.VMEM((8, 32, NB), f32),
            pltpu.VMEM((2, 8, 4, 4, 32, NB), f32),
            pltpu.VMEM((N, N), f32),
            pltpu.VMEM((2, 256, N), f32),
            pltpu.VMEM((256, N), f32),
            pltpu.VMEM((4, 32, N), f32),
            pltpu.VMEM((3, 32, N), f32),
            pltpu.VMEM((256, N), f32),
            pltpu.VMEM((256, N), f32),
            pltpu.VMEM((8, 128), f32),
            pltpu.VMEM((16, 8, 128), f32),
            dma((2, 8)), dma((2, 8)), dma((2, 8)), dma((2, 8)),
            dma((2, 2, 4, 4)), dma((2, 2, 4, 4)),
            dma((4, 8)), dma((4, 8)),
            dma((2,)), dma((2,)),
            dma((2, 4)), dma((2, 4)),
            dma((16, 4)), dma((16, 4)),
            dma((16,)), dma((16,)),
            dma((16,)), dma((16,)),
        ],
        compiler_params=pltpu.CompilerParams(collective_id=0, has_side_effects=True, vmem_limit_bytes=46 << 20),
    )(gradients, momentum, right_basis)


def shards(gradients, momentum, right_basis):
    buffer, right_panel, norm, inner, scaled = panels(gradients, momentum, right_basis)
    new_basis = right_panel / norm
    new_momentum = buffer - (1.0 - DECAY) * inner
    update = (D / math.sqrt(N)) * scaled
    return (new_momentum, new_basis, update)


def solution(mesh):
    return jax.shard_map(
        shards,
        mesh=mesh,
        in_specs=(P("rep", ("row", "col"), None), P(("row", "rep"), "col"), P("col", None)),
        out_specs=(P(("row", "rep"), "col"), P("col", None), P(("row", "rep"), "col")),
        check_vma=False,
    )
```
